256 devices in a mesh: outer: 4 (over x_lo, core), inner: 64 (over z, y, x_hi).
Axes of the slice: x: 4 (x_hi: 2, x_lo: 2; x = x_hi * 2 + x_lo), y: 4, z: 8, core: 2. Of those that a mesh axis runs over, the one named last changes fastest.
Arguments:
- query_rows: bfloat16 [32768, 640], P(('outer', 'inner')), may hold values from -22 to 22
- key_rows: bfloat16 [32768, 128], P(('outer', 'inner')), may hold values from -4.5 to 4.5
- value_rows: bfloat16 [32768, 128], P(('outer', 'inner')), may hold values from -6 to 6
- positions: int32 [32768], P(('outer', 'inner')), may hold values from 0 to 32767, as said below
Outputs:
- attended: bfloat16 [32768, 640], P(('outer', 'inner'))
The draws below stay inside these ranges and needn't reach their ends.
Inputs may be any that keep to these rules, and one draw needn't show every extreme that they name: positions is a permutation of the sequence's positions; each aligned run of 64 rows holds 64 consecutive positions in rising order.
All inputs are finite; a program needn't handle non-finite values.
Results may differ from the reference program's by a relative error of at most 0.0095.
Values may be sent and summed in bfloat16 or wider, within the bound.
No kernel may reach another device: no remote copies, remote signals or barrier semaphores. Data moves between devices by JAX's collectives and lax.ppermute only.
A program may use at most 128 MiB of HBM per device.

```python
import math
import jax
import jax.numpy as jnp
from jax import lax

HD = 128
HEADS = 5
TOKENS = 32768
HALF = 64


def draw_key_rows(key, part):
    key = jax.random.fold_in(key, 3)
    base = jnp.clip(jax.random.normal(key, (TOKENS, HD), jnp.float32), -4.5, 4.5)
    return base.astype(jnp.bfloat16)


def draw_query_rows(key, part):
    key = jax.random.fold_in(key, 5)
    base = jnp.clip(jax.random.normal(key, (TOKENS, HEADS * HD), jnp.float32), -4.5, 4.5)
    return base.astype(jnp.bfloat16)


def draw_positions(key, part):
    key = jax.random.fold_in(key, 7)
    run_count = TOKENS // HALF
    order = jax.random.permutation(key, run_count).astype(jnp.int32)
    index_all = jnp.arange(TOKENS, dtype=jnp.int32)
    return order[index_all // HALF] * HALF + index_all % HALF


def block_levels(own_key, shape, split, low, top_value):
    loudness = 1.0
    for axis_at, shards_of in split:
        steps = jax.random.uniform(jax.random.fold_in(jax.random.fold_in(own_key, 6), axis_at), (shards_of,), jnp.float32, low / len(split), top_value / len(split))
        loudness = loudness * jnp.repeat(jnp.exp(steps), shape[axis_at] // shards_of).reshape((-1,) + (1,) * (len(shape) - 1 - axis_at))
    return loudness


def gaussian(rng, shape, width, limit, split=(), kind=jnp.bfloat16):
    values = width * jax.random.normal(rng, shape, jnp.float32)
    if split:
        values = values * block_levels(rng, shape, split, -0.22, 0.18)
    return jnp.clip(values, -limit, limit).astype(kind)


def setup_inputs(seed: int = 0) -> dict:
    splits = jax.random.split(jax.random.key(seed), 5)
    query_rows = draw_query_rows(jax.random.fold_in(splits[4], 71), 0)
    key_rows = draw_key_rows(jax.random.fold_in(splits[4], 71), 0)
    value_rows = gaussian(splits[2], (TOKENS, HD), 1.0, 6.0, ((0, 256),))
    positions = draw_positions(jax.random.fold_in(splits[4], 71), 0)
    return {"query_rows": query_rows, "key_rows": key_rows, "value_rows": value_rows, "positions": positions}


def reference(query_rows, key_rows, value_rows, positions):
    block_len = math.gcd(TOKENS, 256)
    block_count = TOKENS // block_len
    score_scale = 1.0 / math.sqrt(HD)
    query_blocks = query_rows.reshape(block_count, block_len, HEADS, HD)
    place_blocks = positions.reshape(block_count, block_len)
    key_wide = key_rows.astype(jnp.float32)
    value_wide = value_rows.astype(jnp.float32)

    def one_block(pair):
        query_part, query_place = pair
        scores = jnp.einsum('rhd,kd->hrk', query_part.astype(jnp.float32), key_wide, precision=lax.Precision.HIGHEST) * score_scale
        allowed = positions[None, None, :] <= query_place[None, :, None]
        row_max = lax.optimization_barrier(jnp.max(jnp.where(allowed, scores, -1e+30), axis=-1))
        weights = jnp.where(allowed, jnp.exp(scores - row_max[..., None]), 0.0)
        totals = lax.optimization_barrier(jnp.sum(weights, axis=-1))
        weights_low = weights.astype(jnp.bfloat16).astype(jnp.float32)
        summed = jnp.einsum('hrk,kd->rhd', weights_low, value_wide, precision=lax.Precision.HIGHEST)
        result = summed / jnp.transpose(totals)[..., None]
        return result.reshape(block_len, HEADS * HD).astype(jnp.bfloat16)
    outputs = lax.map(one_block, (query_blocks, place_blocks))
    return outputs.reshape(TOKENS, HEADS * HD)
```

```python
import functools
import math

import jax
import jax.numpy as jnp
from jax import lax
from jax.experimental import pallas as pl
from jax.experimental.pallas import tpu as pltpu
from jax.sharding import Mesh, PartitionSpec as P

HD = 128
HEADS = 5
HALF = 64
TILE_RUNS = 8
TILE = TILE_RUNS * HALF
ROWS = HEADS * HALF
SCALE2 = math.log2(math.e) / math.sqrt(HD)
NEVER = -1e30
SUM_LIMIT = 1e36

AXES = ("xl", "c", "z", "y", "xh")


def nt_dot(a, b):
    return lax.dot_general(a, b, (((1,), (1,)), ((), ())), preferred_element_type=jnp.float32)


def attend_kernel(
    rank_ref, kpos_ref, qpos_ref, below_ref, upto_ref, q_ref, kva_ref, kvb_ref,
    o_ref, l_ref, ks, vs, ps, accs, ms,
):
    shards = kva_ref.shape[0]
    vs[:, HD:] = jnp.ones((vs.shape[0], HD), jnp.bfloat16)

    def place(g, carry):
        for source, ref in enumerate((kva_ref, kvb_ref)):
            for r in range(2):
                i = source * shards * 2 + g * 2 + r
                rank = rank_ref[i]
                at = pl.ds(pl.multiple_of(rank * HALF, HALF), HALF)
                ks[at, :] = ref[g, r * HALF : (r + 1) * HALF, :]
                vs[at, :HD] = ref[g, 128 + r * HALF : 128 + (r + 1) * HALF, :]
                ps[rank] = kpos_ref[i]
        return carry

    lax.fori_loop(0, shards, place, 0, unroll=4)

    lane = lax.broadcasted_iota(jnp.int32, (1, TILE), 1)
    lane_run = lane // HALF
    row_in_run = lax.rem(lax.broadcasted_iota(jnp.int32, (ROWS, 1), 0), HALF)

    def tile_mask(j, q_run):
        base = jnp.zeros((1, TILE), jnp.int32)
        for t in range(TILE_RUNS):
            base = jnp.where(lane_run == t, ps[j * TILE_RUNS + t], base)
        key_place = base * HALF + lax.rem(lane, HALF)
        return key_place <= q_run * HALF + row_in_run

    def one_run(a, carry):
        y, r = a // 2, lax.rem(a, 2)
        q_rows = pl.ds(pl.multiple_of(r * HALF, HALF), HALF)
        q_run = qpos_ref[a]
        below, upto = below_ref[a], upto_ref[a]
        full_tiles = below // TILE_RUNS
        qa = jnp.concatenate(
            [q_ref[y, q_rows, h * HD : (h + 1) * HD] for h in range(HEADS)], axis=0
        )

        def tile_at(j):
            return pl.ds(pl.multiple_of(j * TILE, TILE), TILE)

        def scores(j):
            return nt_dot(qa, ks[tile_at(j), :]) * SCALE2

        def add_up(p, j):
            accs[...] += jnp.dot(
                p.astype(jnp.bfloat16), vs[tile_at(j), :], preferred_element_type=jnp.float32
            )

        accs[...] = jnp.zeros_like(accs)
        ms[...] = jnp.full_like(ms, NEVER)

        @pl.when(upto > 0)
        def _():
            first = nt_dot(qa, ks[:HALF, :]) * SCALE2
            first_lane = lax.broadcasted_iota(jnp.int32, (1, HALF), 1)
            allowed = ps[0] * HALF + first_lane <= q_run * HALF + row_in_run
            ms[...] = jnp.max(jnp.where(allowed, first, NEVER), axis=1, keepdims=True)

            def full(j, c):
                add_up(jnp.exp2(scores(j) - ms[...]), j)
                return c

            lax.fori_loop(0, full_tiles, full, 0)

            @pl.when(upto > full_tiles * TILE_RUNS)
            def _():
                s = scores(full_tiles)
                p = jnp.where(tile_mask(full_tiles, q_run), jnp.exp2(s - ms[...]), 0.0)
                add_up(p, full_tiles)

            fits = jnp.max(jnp.where(accs[:, HD:] < SUM_LIMIT, 0, 1))

            @pl.when(fits > 0)
            def _():
                accs[...] = jnp.zeros_like(accs)
                ms[...] = jnp.full_like(ms, NEVER)

                def online(j, c):
                    allowed = tile_mask(j, q_run)
                    s = scores(j)
                    m_old = ms[...]
                    m_new = jnp.maximum(
                        m_old, jnp.max(jnp.where(allowed, s, NEVER), axis=1, keepdims=True)
                    )
                    accs[...] = accs[...] * jnp.exp2(m_old - m_new)
                    ms[...] = m_new
                    add_up(jnp.where(allowed, jnp.exp2(s - m_new), 0.0), j)
                    return c

                lax.fori_loop(0, pl.cdiv(upto, TILE_RUNS), online, 0)

        total = accs[:, HD:]
        some = total > 0
        safe = jnp.where(some, total, 1.0)
        out = (accs[:, :HD] / safe).astype(jnp.bfloat16)
        level = jnp.where(some, ms[...] + jnp.log2(safe), NEVER)
        sub = lax.broadcasted_iota(jnp.int32, (HALF, HD), 0)
        spot = lax.broadcasted_iota(jnp.int32, (HALF, HD), 1) == sub + r * HALF
        old = l_ref[y]
        mine = lax.broadcasted_iota(jnp.int32, (1, HD), 1) // HALF == r
        rows = []
        for h in range(HEADS):
            part = slice(h * HALF, (h + 1) * HALF)
            o_ref[y, q_rows, h * HD : (h + 1) * HD] = out[part]
            rows.append(jnp.sum(jnp.where(spot, level[part], 0.0), axis=0, keepdims=True))
        rows.append(jnp.zeros((8 - HEADS, HD), jnp.float32))
        l_ref[y] = jnp.where(mine, jnp.concatenate(rows, axis=0), old)
        return carry

    lax.fori_loop(0, 8, one_run, 0)


def attend(rank, kpos, qpos, below, upto, q, kva, kvb):
    runs = rank.shape[0]
    smem = pl.BlockSpec(memory_space=pltpu.SMEM)
    vmem = pl.BlockSpec(memory_space=pltpu.VMEM)
    return pl.pallas_call(
        attend_kernel,
        out_shape=(
            jax.ShapeDtypeStruct(q.shape, jnp.bfloat16),
            jax.ShapeDtypeStruct((q.shape[0], 8, 128), jnp.float32),
        ),
        in_specs=[smem] * 5 + [vmem] * 3,
        out_specs=(vmem, vmem),
        scratch_shapes=[
            pltpu.VMEM((runs * HALF, HD), jnp.bfloat16),
            pltpu.VMEM((runs * HALF, 2 * HD), jnp.bfloat16),
            pltpu.SMEM((runs,), jnp.int32),
            pltpu.VMEM((ROWS, 2 * HD), jnp.float32),
            pltpu.VMEM((ROWS, 1), jnp.float32),
        ],
        compiler_params=pltpu.CompilerParams(vmem_limit_bytes=40 * 1024 * 1024),
        name="attend",
    )(rank, kpos, qpos, below, upto, q, kva, kvb)


def combine_kernel(o_ref, l_ref, out_ref):
    parts = o_ref.shape[0]
    levels = [l_ref[j] for j in range(parts)]
    top = functools.reduce(jnp.maximum, levels)
    weights = [jnp.exp2(level - top) for level in levels]
    total = functools.reduce(jnp.add, weights)
    columns = [jnp.transpose(w / total) for w in weights]
    for h in range(HEADS):
        at = slice(h * HD, (h + 1) * HD)
        acc = o_ref[0, :, at].astype(jnp.float32) * columns[0][:, h : h + 1]
        for j in range(1, parts):
            acc += o_ref[j, :, at].astype(jnp.float32) * columns[j][:, h : h + 1]
        out_ref[:, at] = acc.astype(jnp.bfloat16)


def combine(o, l):
    vmem = pl.BlockSpec(memory_space=pltpu.VMEM)
    return pl.pallas_call(
        combine_kernel,
        out_shape=jax.ShapeDtypeStruct(o.shape[1:], jnp.bfloat16),
        in_specs=[vmem, vmem],
        out_specs=vmem,
        name="combine",
    )(o, l)


def spread(x, axis, n):
    return lax.all_to_all(jnp.broadcast_to(x[None], (n,) + x.shape), axis, 0, 0)


def swap_cores(x):
    return lax.ppermute(x, "c", [(0, 1), (1, 0)])


def local(query_rows, key_rows, value_rows, positions):
    kv = jnp.concatenate([key_rows, value_rows], axis=0)
    run_no = positions[::HALF] // HALF
    run_tile = jnp.broadcast_to(jnp.pad(run_no, (0, 126))[None], (8, 128))

    kv_z = spread(kv, "z", 8)
    q_all = spread(query_rows, "y", 4)
    q_runs = spread(run_tile, "y", 4)[:, 0, :2].reshape(8)
    k_runs_own = spread(run_tile, ("xl", "xh", "z"), 32)[:, 0, :2].reshape(64)
    k_runs = jnp.concatenate([k_runs_own, swap_cores(k_runs_own)])
    rank = jnp.sum(k_runs[None, :] < k_runs[:, None], axis=1, dtype=jnp.int32)
    below = jnp.sum(k_runs[None, :] < q_runs[:, None], axis=1, dtype=jnp.int32)
    upto = jnp.sum(k_runs[None, :] <= q_runs[:, None], axis=1, dtype=jnp.int32)

    kv_own = spread(kv_z, ("xl", "xh"), 4).reshape(32, 256, HD)
    kv_other = swap_cores(kv_own)
    o, l = attend(rank, k_runs, q_runs, below, upto, q_all, kv_own, kv_other)
    o = lax.all_to_all(o, "y", 0, 0)
    l = lax.all_to_all(l, "y", 0, 0)
    return combine(o, l)


def solution(mesh):
    fine = Mesh(mesh.devices.reshape(2, 2, 8, 4, 2), AXES)
    rows = P(AXES, None)
    return jax.shard_map(
        local, mesh=fine, in_specs=(rows, rows, rows, P(AXES)), out_specs=rows, check_vma=False
    )
```

```python
import functools
import math

import jax
import jax.numpy as jnp
from jax import lax
from jax.experimental import pallas as pl
from jax.experimental.pallas import tpu as pltpu
from jax.sharding import Mesh, PartitionSpec as P

HD = 128
HEADS = 5
HALF = 64
LOCAL = 128
QRUNS = 8
BLOCK_RUNS = 4
BLOCK = BLOCK_RUNS * HALF
COLS = 4 * HALF
SLABS = QRUNS * HEADS * HALF // COLS
ACC_ROWS = HD + 16
GROUP = 8
NOTE = 16
FACTS = 32
SCALE2 = math.log2(math.e) / math.sqrt(HD)
NEVER = -1e30
SHUT = 1e30
SUM_LIMIT = 1e36

AXES = ("xl", "c", "z", "y", "xh")
STATE = (
    jax.ShapeDtypeStruct((QRUNS, HD), jnp.float32),
    jax.ShapeDtypeStruct((SLABS + 1, HD, COLS), jnp.bfloat16),
    jax.ShapeDtypeStruct((SLABS + 1, ACC_ROWS, COLS), jnp.float32),
    jax.ShapeDtypeStruct((SLABS + 1, 1, COLS), jnp.float32),
)


def runs_of_slab(n):
    return [n] * 4 if n < QRUNS else [(n - QRUNS) * 4 + w for w in range(4)]


def head_of_slab(n, w):
    return w if n < QRUNS else HEADS - 1


def attend_kernel(first, last, n_kv, *refs):
    refs = list(refs)

    def take(n):
        got = refs[:n]
        del refs[:n]
        return got

    if first:
        q_refs = take(QRUNS // 2)
    (slot_ref,) = take(1)
    kv_refs = take(n_kv)
    if not first:
        seen_ref, qnum_in, qt, accs_in, ms_in = take(5)
    (o_ref,) = take(1)
    if first:
        qnum, qt, accs, ms = take(4)
    elif last:
        accs, ms = take(2)
    else:
        accs, ms = take(2)
    ks, vs, vt, s0, s1, places, qrun, facts_v, facts, ps, item_slab, item_block, facts_sem = refs
    runs = 2 * sum(ref.shape[0] for ref in kv_refs)
    blocks = runs // BLOCK_RUNS

    def numbers(note):
        note = note.astype(jnp.float32)
        return note[0:1] * 16 + note[1:2], note[2:3] * 16 + note[3:4]

    i = 0
    for ref in kv_refs:
        for g in range(ref.shape[0]):
            one, two = numbers(ref[g, 2 * LOCAL :, :])
            places[i : i + 1, :] = one
            places[i + 1 : i + 2, :] = two
            i += 2
    places[runs:, :] = jnp.full((places.shape[0] - runs, HD), 1e6, jnp.float32)
    down = places[...]
    across = jnp.transpose(down)
    if first:
        q_rows = [n for ref in q_refs for n in numbers(ref[LOCAL:, :HD])]
        qnum[...] = jnp.concatenate(q_rows, axis=0)
    else:
        q_rows = [qnum_in[a : a + 1, :] for a in range(QRUNS)]

    def count(holds):
        return jnp.sum(jnp.where(holds, 1.0, 0.0), axis=0, keepdims=True)

    facts_v[...] = jnp.concatenate(
        [count(down < across), across[0:1]]
        + q_rows
        + [count(down < q) for q in q_rows]
        + [count(down <= q) for q in q_rows]
        + [jnp.zeros((FACTS - 2 - 3 * QRUNS, HD), jnp.float32)],
        axis=0,
    ).astype(jnp.int32)
    copy = pltpu.make_async_copy(facts_v, facts, facts_sem)
    copy.start()

    group = lax.broadcasted_iota(jnp.int32, (1, HD), 1) // HALF
    for n in range(SLABS):
        of = runs_of_slab(n)
        halves = [jnp.where(group == 0, q_rows[of[v]], q_rows[of[v + 1]]) for v in (0, 2)]
        qrun[n] = jnp.concatenate(halves, axis=1).astype(jnp.int32)
    qrun[SLABS] = jnp.zeros((1, COLS), jnp.int32)
    inside = lax.rem(lax.broadcasted_iota(jnp.int32, (1, COLS), 1), HALF)

    if first:
        for n in range(SLABS):
            rows = []
            for w, a in enumerate(runs_of_slab(n)):
                h = head_of_slab(n, w)
                rows.append(
                    q_refs[a // 2][(a % 2) * HALF : (a % 2 + 1) * HALF, h * HD : (h + 1) * HD]
                )
            slab = jnp.concatenate(rows, axis=0).astype(jnp.float32)
            qt[n] = jnp.transpose(slab).astype(jnp.bfloat16)
        qt[SLABS] = jnp.zeros((HD, COLS), jnp.bfloat16)

    def load_state():
        if first:
            accs[...] = jnp.zeros_like(accs)
            ms[...] = jnp.full_like(ms, NEVER)
        else:
            accs[...] = accs_in[...]
            ms[...] = ms_in[...]
        ms[SLABS] = jnp.zeros((1, COLS), jnp.float32)

    load_state()
    copy.wait()

    class Column:
        def __init__(self, start):
            self.start = start

        def __getitem__(self, a):
            return facts[self.start + a, 0]

    below, upto = Column(2 + QRUNS), Column(2 + 2 * QRUNS)

    i = 0
    for ref in kv_refs:
        for g in range(ref.shape[0]):
            for r in range(2):
                rank = facts[0, i]
                at = pl.ds(pl.multiple_of(rank * HALF, HALF), HALF)
                ks[at, :] = ref[g, r * HALF : (r + 1) * HALF, :]
                vs[at, :] = ref[g, LOCAL + r * HALF : LOCAL + (r + 1) * HALF, :]
                ps[rank] = facts[1, i]
                i += 1
    for b in range(blocks):
        turned = jnp.transpose(vs[b * BLOCK : (b + 1) * BLOCK, :].astype(jnp.float32))
        vt[b, :HD, :] = turned.astype(jnp.bfloat16)
        vt[b, HD:, :] = jnp.ones((ACC_ROWS - HD, BLOCK), jnp.bfloat16)

    down_run = lax.broadcasted_iota(jnp.int32, (HALF, COLS), 0)

    def first_shift():
        for n in range(SLABS):
            s = jnp.dot(ks[:HALF, :], qt[n], preferred_element_type=jnp.float32) * SCALE2
            ok = down_run <= (qrun[n] - ps[0]) * HALF + inside
            top = jnp.max(jnp.where(ok, s, NEVER), axis=0, keepdims=True)
            ms[n] = top if first else jnp.where(ms[n] > 0.5 * NEVER, ms[n], top)

    if first:
        first_shift()
    else:
        fewest = functools.reduce(jnp.minimum, [seen_ref[a] for a in range(QRUNS)])
        pl.when(fewest == 0)(first_shift)

    count = 0
    for n in range(SLABS):

        def add(b, k, n=n):
            item_slab[k] = n
            item_block[k] = b
            return k + 1

        end = functools.reduce(jnp.maximum, [below[a] for a in set(runs_of_slab(n))])
        count = lax.fori_loop(0, pl.cdiv(end, BLOCK_RUNS), add, count)
    for e in range(2 * GROUP):
        item_slab[count + e] = SLABS
        item_block[count + e] = 0

    def score(n, b):
        at = pl.ds(pl.multiple_of(b * BLOCK, BLOCK), BLOCK)
        return jnp.dot(ks[at, :], qt[n], preferred_element_type=jnp.float32)

    def consume(s, k):
        n, b = item_slab[k], item_block[k]
        mine, shift = qrun[n], ms[n]
        parts = []
        for t in range(BLOCK_RUNS):
            low = jnp.where(ps[b * BLOCK_RUNS + t] < mine, shift, SHUT)
            p = jnp.exp2(s[t * HALF : (t + 1) * HALF] * SCALE2 - low)
            parts.append(p.astype(jnp.bfloat16))
        p = jnp.concatenate(parts, axis=0)
        accs[n] += jnp.dot(vt[b], p, preferred_element_type=jnp.float32)

    def phase(now, later, base):
        for g in range(GROUP):
            k = base + GROUP + g
            later[g] = score(item_slab[k], item_block[k])
            consume(now[g], base + g)

    @pl.when(count > 0)
    def _():
        for g in range(GROUP):
            s0[g] = score(item_slab[g], item_block[g])
        phases = pl.cdiv(count, GROUP)

        def two(k, c):
            phase(s0, s1, 2 * GROUP * k)
            phase(s1, s0, 2 * GROUP * k + GROUP)
            return c

        lax.fori_loop(0, phases // 2, two, 0)

        @pl.when(lax.rem(phases, 2) == 1)
        def _():
            for g in range(GROUP):
                consume(s0[g], (phases - 1) * GROUP + g)

    def diagonal(a, c):
        @pl.when(upto[a] > below[a])
        def _():
            at = pl.ds(pl.multiple_of(below[a] * HALF, HALF), HALF)
            for n in (a, QRUNS + a // 4):
                s = jnp.dot(ks[at, :], qt[n], preferred_element_type=jnp.float32)
                ok = jnp.logical_and(qrun[n] == facts[2 + a, 0], down_run <= inside)
                p = jnp.where(ok, jnp.exp2(s * SCALE2 - ms[n]), 0.0).astype(jnp.bfloat16)
                accs[n, :HD, :] += lax.dot_general(
                    vs[at, :], p, (((0,), (0,)), ((), ())), preferred_element_type=jnp.float32
                )
                accs[n, HD:, :] += jnp.sum(p.astype(jnp.float32), axis=0, keepdims=True)

        return c

    lax.fori_loop(0, QRUNS, diagonal, 0)

    worst = jnp.zeros((1, COLS), jnp.int32)
    for n in range(SLABS):
        worst = jnp.maximum(worst, jnp.where(accs[n, HD : HD + 1, :] < SUM_LIMIT, 0, 1))

    @pl.when(jnp.max(worst) > 0)
    def _():
        load_state()

        def per_slab(n, c):
            def online(b, c):
                s = score(n, b) * SCALE2
                keep = jnp.concatenate(
                    [
                        jnp.where(
                            down_run <= (qrun[n] - ps[b * BLOCK_RUNS + t]) * HALF + inside, 0.0, 1.0
                        )
                        for t in range(BLOCK_RUNS)
                    ],
                    axis=0,
                )
                old = ms[n]
                s = jnp.where(keep > 0, NEVER, s)
                new = jnp.maximum(old, jnp.max(s, axis=0, keepdims=True))
                p = jnp.where(keep > 0, 0.0, jnp.exp2(s - new))
                ms[n] = new
                accs[n] = accs[n] * jnp.exp2(old - new) + jnp.dot(
                    vt[b], p.astype(jnp.bfloat16), preferred_element_type=jnp.float32
                )
                return c

            return lax.fori_loop(0, blocks, online, c)

        lax.fori_loop(0, SLABS, per_slab, 0)

    if not last:
        for a in range(QRUNS):
            o_ref[a] = upto[a] if first else seen_ref[a] + upto[a]
        return
    levels = []
    for n in range(SLABS):
        total = accs[n, HD : HD + 1, :]
        some = total > 0
        safe = jnp.where(some, total, 1.0)
        levels.append(jnp.where(some, ms[n] + jnp.log2(safe), NEVER))
        out = jnp.transpose(accs[n, :HD, :] / safe).astype(jnp.bfloat16)
        for w, a in enumerate(runs_of_slab(n)):
            h = head_of_slab(n, w)
            o_ref[
                slot_ref[a // 2], (a % 2) * HALF : (a % 2 + 1) * HALF, h * HD : (h + 1) * HD
            ] = out[w * HALF : (w + 1) * HALF]
    low_half = lax.broadcasted_iota(jnp.int32, (8, HD), 1) < HALF

    def piece(n, v):
        return jnp.broadcast_to(levels[n][:, v * HD : (v + 1) * HD], (8, HD))

    for y in range(QRUNS // 2):
        rows = []
        for h in range(HEADS - 1):
            one, two = piece(2 * y, h // 2), piece(2 * y + 1, h // 2)
            if h % 2:
                one = pltpu.roll(one, HALF, 1)
            else:
                two = pltpu.roll(two, HALF, 1)
            rows.append(jnp.where(low_half, one, two))
        rows.append(piece(QRUNS + y // 2, y % 2))
        level = jnp.concatenate(rows, axis=1)[:1]
        high = level.astype(jnp.bfloat16).astype(jnp.float32)
        middle = (level - high).astype(jnp.bfloat16).astype(jnp.float32)
        low = level - high - middle
        note = jnp.concatenate(
            [high, middle, low, jnp.zeros((NOTE - 3, HEADS * HD), jnp.float32)], axis=0
        )
        o_ref[slot_ref[y], LOCAL:, :] = note.astype(jnp.bfloat16)


def attend(slots, queries, blocks, state, last, name):
    first = not state
    runs = 2 * sum(b.shape[0] for b in blocks)
    smem = pl.BlockSpec(memory_space=pltpu.SMEM)
    vmem = pl.BlockSpec(memory_space=pltpu.VMEM)
    items = SLABS * (runs // BLOCK_RUNS) + 2 * GROUP + 8
    scratch = [
        pltpu.VMEM((runs * HALF, HD), jnp.bfloat16),
        pltpu.VMEM((runs * HALF, HD), jnp.bfloat16),
        pltpu.VMEM((runs // BLOCK_RUNS, ACC_ROWS, BLOCK), jnp.bfloat16),
        pltpu.VMEM((GROUP, BLOCK, COLS), jnp.float32),
        pltpu.VMEM((GROUP, BLOCK, COLS), jnp.float32),
        pltpu.VMEM((HD, HD), jnp.float32),
        pltpu.VMEM((SLABS + 1, 1, COLS), jnp.int32),
        pltpu.VMEM((FACTS, HD), jnp.int32),
        pltpu.SMEM((FACTS, HD), jnp.int32),
        pltpu.SMEM((runs,), jnp.int32),
        pltpu.SMEM((items,), jnp.int32),
        pltpu.SMEM((items,), jnp.int32),
        pltpu.SemaphoreType.DMA(()),
    ]
    seen = jax.ShapeDtypeStruct((QRUNS,), jnp.int32)
    if last:
        out_shape = jax.ShapeDtypeStruct((QRUNS // 2, LOCAL + NOTE, HEADS * HD), jnp.bfloat16)
        out_specs = vmem
        scratch = [pltpu.VMEM(s.shape, s.dtype) for s in STATE[2:]] + scratch
    else:
        out_shape = (seen,) + (STATE if first else STATE[2:])
        out_specs = (smem,) + (vmem,) * (len(out_shape) - 1)
    pairs = QRUNS * HEADS * HALF * runs * HALF // 2
    got = pl.pallas_call(
        functools.partial(attend_kernel, first, last, len(blocks)),
        out_shape=out_shape,
        in_specs=([vmem] * len(queries) if first else [])
        + [smem]
        + [vmem] * len(blocks)
        + ([] if first else [smem] + [vmem] * len(STATE)),
        out_specs=out_specs,
        scratch_shapes=scratch,
        compiler_params=pltpu.CompilerParams(vmem_limit_bytes=20 * 1024 * 1024),
        cost_estimate=pl.CostEstimate(
            flops=4 * pairs * HD, bytes_accessed=runs * HALF * HD * 4, transcendentals=pairs
        ),
        name=name,
    )(*(queries if first else []), slots, *blocks, *state)
    if last:
        return got
    return got if first else (got[0],) + state[1:3] + got[1:]


def combine_kernel(o_ref, out_ref):
    parts = o_ref.shape[0]
    levels = []
    for j in range(parts):
        note = o_ref[j, LOCAL:, :].astype(jnp.float32)
        row = note[0:1] + note[1:2] + note[2:3]
        heads = [row[:, h * HD : (h + 1) * HD] for h in range(HEADS)]
        levels.append(
            jnp.concatenate(heads + [jnp.zeros((8 - HEADS, HD), jnp.float32)], axis=0)
        )
    top = functools.reduce(jnp.maximum, levels)
    weights = [jnp.exp2(level - top) for level in levels]
    total = functools.reduce(jnp.add, weights)
    columns = [jnp.transpose(w / total) for w in weights]
    for h in range(HEADS):
        at = slice(h * HD, (h + 1) * HD)
        acc = o_ref[0, :LOCAL, at].astype(jnp.float32) * columns[0][:, h : h + 1]
        for j in range(1, parts):
            acc += o_ref[j, :LOCAL, at].astype(jnp.float32) * columns[j][:, h : h + 1]
        out_ref[:, at] = acc.astype(jnp.bfloat16)


def combine(o):
    vmem = pl.BlockSpec(memory_space=pltpu.VMEM)
    return pl.pallas_call(
        combine_kernel,
        out_shape=jax.ShapeDtypeStruct((LOCAL, HEADS * HD), jnp.bfloat16),
        in_specs=[vmem],
        out_specs=vmem,
        compiler_params=pltpu.CompilerParams(vmem_limit_bytes=8 * 1024 * 1024),
        name="combine",
    )(o)


def shift(x, axis, n, by):
    return lax.ppermute(x, axis, [(i, (i + by) % n) for i in range(n)])


def after(arrays, token):
    def nothing(token_ref, *refs):
        del token_ref, refs

    whole = pl.BlockSpec(memory_space=pl.ANY)
    return pl.pallas_call(
        nothing,
        out_shape=[jax.ShapeDtypeStruct(x.shape, x.dtype) for x in arrays],
        in_specs=[whole] * (1 + len(arrays)),
        out_specs=[whole] * len(arrays),
        input_output_aliases={i + 1: i for i in range(len(arrays))},
        compiler_params=pltpu.CompilerParams(vmem_limit_bytes=1024 * 1024),
        name="after",
    )(token, *arrays)


def note_of(run_no, width):
    digits = jnp.stack([run_no // 16, run_no % 16], axis=1).reshape(4, 1)
    digits = jnp.pad(digits, ((0, NOTE - 4), (0, 0))).astype(jnp.bfloat16)
    return jnp.broadcast_to(digits, (NOTE, width))


def local(query_rows, key_rows, value_rows, positions):
    run_no = positions[::HALF] // HALF
    kv = jnp.concatenate([key_rows, value_rows, note_of(run_no, HD)], axis=0)
    qn = jnp.concatenate([query_rows, note_of(run_no, HEADS * HD)], axis=0)

    queries = [qn] + [shift(qn, "y", 4, k) for k in (1, 2, 3)]
    slots = lax.rem(lax.axis_index("y") + 4 - jnp.arange(4, dtype=jnp.int32), 4)

    copies = jnp.broadcast_to(kv[None], (4,) + kv.shape)
    (copies,) = after([copies], qn)
    own = lax.all_to_all(copies, ("xl", "xh"), 0, 0)

    def attend_to(blocks, state, step, last=False):
        both = [x for b in blocks for x in (b, shift(b, "c", 2, 1))]
        return attend(slots, queries, both, state, last, f"attend_{step}")

    def pass_on(pair):
        return [shift(pair[0], "z", 8, 1), shift(pair[1], "z", 8, -1)]

    one = pass_on([own, own])
    two = pass_on(one)
    state = attend_to([own], (), 0)
    two = after(two, state[0])
    three = pass_on(two)
    state = attend_to(one, state, 1)
    three = after(three, state[0])
    four = pass_on([three[0][:2], three[1][2:]])
    state = attend_to(two, state, 2)
    four = after(four, state[0])
    out = attend_to(three + four, state, 3, last=True)
    return combine(lax.all_to_all(out, "y", 0, 0))


def solution(mesh):
    fine = Mesh(mesh.devices.reshape(2, 2, 8, 4, 2), AXES)
    rows = P(AXES, None)
    return jax.shard_map(
        local, mesh=fine, in_specs=(rows, rows, rows, P(AXES)), out_specs=rows, check_vma=False
    )
```

```python
import functools
import math

import jax
import jax.numpy as jnp
from jax import lax
from jax.experimental import pallas as pl
from jax.experimental.pallas import tpu as pltpu
from jax.sharding import Mesh, PartitionSpec as P

HD = 128
HEADS = 5
HALF = 64
LOCAL = 128
QRUNS = 8
BLOCK_RUNS = 4
BLOCK = BLOCK_RUNS * HALF
COLS = 4 * HALF
SLABS = QRUNS * HEADS * HALF // COLS
ACC_ROWS = HD + 16
GROUP = 8
NOTE = 16
FACTS = 32
SCALE2 = math.log2(math.e) / math.sqrt(HD)
NEVER = -1e30
SHUT = 1e30
SUM_LIMIT = 1e36

AXES = ("xl", "c", "z", "y", "xh")
STATE = (
    jax.ShapeDtypeStruct((QRUNS, HD), jnp.float32),
    jax.ShapeDtypeStruct((SLABS + 1, HD, COLS), jnp.bfloat16),
    jax.ShapeDtypeStruct((SLABS + 1, ACC_ROWS, COLS), jnp.float32),
    jax.ShapeDtypeStruct((SLABS + 1, 1, COLS), jnp.float32),
)


def runs_of_slab(n):
    return [n] * 4 if n < QRUNS else [(n - QRUNS) * 4 + w for w in range(4)]


def head_of_slab(n, w):
    return w if n < QRUNS else HEADS - 1


def attend_kernel(first, ys, n_kv, n_wait, *refs):
    refs = list(refs)
    last = ys is not None
    mine = list(ys) if last else list(range(QRUNS // 2))
    my_runs = [2 * y + r for y in mine for r in range(2)]
    my_slabs = [n for n in range(SLABS) if runs_of_slab(n)[0] in my_runs]

    def take(n):
        got = refs[:n]
        del refs[:n]
        return got

    if first:
        q_refs = take(QRUNS // 2)
    kv_refs = take(n_kv)
    if not first:
        seen_ref, qnum_in, qt, accs_in, ms_in = take(5)
    take(n_wait)
    if last:
        o_refs = take(len(mine))
    else:
        (o_ref,) = take(1)
    if first:
        qnum, qt, accs, ms = take(4)
    elif last:
        accs, ms = take(2)
    else:
        accs, ms = take(2)
    ks, vs, vt, s0, s1, places, qrun, facts_v, facts, ps, item_slab, item_block, facts_sem = refs
    runs = 2 * sum(ref.shape[0] for ref in kv_refs)
    blocks = runs // BLOCK_RUNS

    def numbers(note):
        note = note.astype(jnp.float32)
        return note[0:1] * 16 + note[1:2], note[2:3] * 16 + note[3:4]

    i = 0
    for ref in kv_refs:
        for g in range(ref.shape[0]):
            one, two = numbers(ref[g, 2 * LOCAL :, :])
            places[i : i + 1, :] = one
            places[i + 1 : i + 2, :] = two
            i += 2
    places[runs:, :] = jnp.full((places.shape[0] - runs, HD), 1e6, jnp.float32)
    down = places[...]
    across = jnp.transpose(down)
    if first:
        q_rows = [n for ref in q_refs for n in numbers(ref[LOCAL:, :HD])]
        qnum[...] = jnp.concatenate(q_rows, axis=0)
    else:
        q_rows = [qnum_in[a : a + 1, :] for a in range(QRUNS)]

    def count(holds):
        return jnp.sum(jnp.where(holds, 1.0, 0.0), axis=0, keepdims=True)

    facts_v[...] = jnp.concatenate(
        [count(down < across), across[0:1]]
        + q_rows
        + [count(down < q) for q in q_rows]
        + [count(down <= q) for q in q_rows]
        + [jnp.zeros((FACTS - 2 - 3 * QRUNS, HD), jnp.float32)],
        axis=0,
    ).astype(jnp.int32)
    copy = pltpu.make_async_copy(facts_v, facts, facts_sem)
    copy.start()

    group = lax.broadcasted_iota(jnp.int32, (1, HD), 1) // HALF
    for n in range(SLABS):
        of = runs_of_slab(n)
        halves = [jnp.where(group == 0, q_rows[of[v]], q_rows[of[v + 1]]) for v in (0, 2)]
        qrun[n] = jnp.concatenate(halves, axis=1).astype(jnp.int32)
    qrun[SLABS] = jnp.zeros((1, COLS), jnp.int32)
    inside = lax.rem(lax.broadcasted_iota(jnp.int32, (1, COLS), 1), HALF)

    if first:
        for n in range(SLABS):
            rows = []
            for w, a in enumerate(runs_of_slab(n)):
                h = head_of_slab(n, w)
                rows.append(
                    q_refs[a // 2][(a % 2) * HALF : (a % 2 + 1) * HALF, h * HD : (h + 1) * HD]
                )
            slab = jnp.concatenate(rows, axis=0).astype(jnp.float32)
            qt[n] = jnp.transpose(slab).astype(jnp.bfloat16)
        qt[SLABS] = jnp.zeros((HD, COLS), jnp.bfloat16)

    def load_state():
        if first:
            accs[...] = jnp.zeros_like(accs)
            ms[...] = jnp.full_like(ms, NEVER)
        else:
            for n in my_slabs:
                accs[n] = accs_in[n]
                ms[n] = ms_in[n]
            accs[SLABS] = jnp.zeros((ACC_ROWS, COLS), jnp.float32)
        ms[SLABS] = jnp.zeros((1, COLS), jnp.float32)

    load_state()
    copy.wait()

    class Column:
        def __init__(self, start):
            self.start = start

        def __getitem__(self, a):
            return facts[self.start + a, 0]

    below, upto = Column(2 + QRUNS), Column(2 + 2 * QRUNS)

    i = 0
    for ref in kv_refs:
        for g in range(ref.shape[0]):
            for r in range(2):
                rank = facts[0, i]
                at = pl.ds(pl.multiple_of(rank * HALF, HALF), HALF)
                ks[at, :] = ref[g, r * HALF : (r + 1) * HALF, :]
                vs[at, :] = ref[g, LOCAL + r * HALF : LOCAL + (r + 1) * HALF, :]
                ps[rank] = facts[1, i]
                i += 1
    for b in range(blocks):
        turned = jnp.transpose(vs[b * BLOCK : (b + 1) * BLOCK, :].astype(jnp.float32))
        vt[b, :HD, :] = turned.astype(jnp.bfloat16)
        vt[b, HD:, :] = jnp.ones((ACC_ROWS - HD, BLOCK), jnp.bfloat16)

    down_run = lax.broadcasted_iota(jnp.int32, (HALF, COLS), 0)

    def first_shift():
        for n in my_slabs:
            s = jnp.dot(ks[:HALF, :], qt[n], preferred_element_type=jnp.float32) * SCALE2
            ok = down_run <= (qrun[n] - ps[0]) * HALF + inside
            top = jnp.max(jnp.where(ok, s, NEVER), axis=0, keepdims=True)
            ms[n] = top if first else jnp.where(ms[n] > 0.5 * NEVER, ms[n], top)

    if first:
        first_shift()
    else:
        fewest = functools.reduce(jnp.minimum, [seen_ref[a] for a in my_runs])
        pl.when(fewest == 0)(first_shift)

    count = 0
    for n in my_slabs:

        def add(b, k, n=n):
            item_slab[k] = n
            item_block[k] = b
            return k + 1

        end = functools.reduce(jnp.maximum, [below[a] for a in set(runs_of_slab(n))])
        count = lax.fori_loop(0, pl.cdiv(end, BLOCK_RUNS), add, count)
    for e in range(2 * GROUP):
        item_slab[count + e] = SLABS
        item_block[count + e] = 0

    def score(n, b):
        at = pl.ds(pl.multiple_of(b * BLOCK, BLOCK), BLOCK)
        return jnp.dot(ks[at, :], qt[n], preferred_element_type=jnp.float32)

    def consume(s, k):
        n, b = item_slab[k], item_block[k]
        mine, shift = qrun[n], ms[n]
        parts = []
        for t in range(BLOCK_RUNS):
            low = jnp.where(ps[b * BLOCK_RUNS + t] < mine, shift, SHUT)
            p = jnp.exp2(s[t * HALF : (t + 1) * HALF] * SCALE2 - low)
            parts.append(p.astype(jnp.bfloat16))
        p = jnp.concatenate(parts, axis=0)
        accs[n] += jnp.dot(vt[b], p, preferred_element_type=jnp.float32)

    def phase(now, later, base):
        for g in range(GROUP):
            k = base + GROUP + g
            later[g] = score(item_slab[k], item_block[k])
            consume(now[g], base + g)

    @pl.when(count > 0)
    def _():
        for g in range(GROUP):
            s0[g] = score(item_slab[g], item_block[g])
        phases = pl.cdiv(count, GROUP)

        def two(k, c):
            phase(s0, s1, 2 * GROUP * k)
            phase(s1, s0, 2 * GROUP * k + GROUP)
            return c

        lax.fori_loop(0, phases // 2, two, 0)

        @pl.when(lax.rem(phases, 2) == 1)
        def _():
            for g in range(GROUP):
                consume(s0[g], (phases - 1) * GROUP + g)

    def diagonal(a, c):
        @pl.when(upto[a] > below[a])
        def _():
            at = pl.ds(pl.multiple_of(below[a] * HALF, HALF), HALF)
            for n in (a, QRUNS + a // 4):
                s = jnp.dot(ks[at, :], qt[n], preferred_element_type=jnp.float32)
                ok = jnp.logical_and(qrun[n] == facts[2 + a, 0], down_run <= inside)
                p = jnp.where(ok, jnp.exp2(s * SCALE2 - ms[n]), 0.0).astype(jnp.bfloat16)
                accs[n, :HD, :] += lax.dot_general(
                    vs[at, :], p, (((0,), (0,)), ((), ())), preferred_element_type=jnp.float32
                )
                accs[n, HD:, :] += jnp.sum(p.astype(jnp.float32), axis=0, keepdims=True)

        return c

    lax.fori_loop(my_runs[0], my_runs[-1] + 1, diagonal, 0)

    worst = jnp.zeros((1, COLS), jnp.int32)
    for n in my_slabs:
        worst = jnp.maximum(worst, jnp.where(accs[n, HD : HD + 1, :] < SUM_LIMIT, 0, 1))

    @pl.when(jnp.max(worst) > 0)
    def _():
        load_state()

        def per_slab(n, c):
            def online(b, c):
                s = score(n, b) * SCALE2
                keep = jnp.concatenate(
                    [
                        jnp.where(
                            down_run <= (qrun[n] - ps[b * BLOCK_RUNS + t]) * HALF + inside, 0.0, 1.0
                        )
                        for t in range(BLOCK_RUNS)
                    ],
                    axis=0,
                )
                old = ms[n]
                s = jnp.where(keep > 0, NEVER, s)
                new = jnp.maximum(old, jnp.max(s, axis=0, keepdims=True))
                p = jnp.where(keep > 0, 0.0, jnp.exp2(s - new))
                ms[n] = new
                accs[n] = accs[n] * jnp.exp2(old - new) + jnp.dot(
                    vt[b], p.astype(jnp.bfloat16), preferred_element_type=jnp.float32
                )
                return c

            return lax.fori_loop(0, blocks, online, c)

        for n in my_slabs:
            per_slab(n, 0)

    if not last:
        for a in range(QRUNS):
            o_ref[a] = upto[a] if first else seen_ref[a] + upto[a]
        return
    levels = {}
    for n in my_slabs:
        total = accs[n, HD : HD + 1, :]
        some = total > 0
        safe = jnp.where(some, total, 1.0)
        levels[n] = jnp.where(some, ms[n] + jnp.log2(safe), NEVER)
        out = jnp.transpose(accs[n, :HD, :] / safe).astype(jnp.bfloat16)
        for w, a in enumerate(runs_of_slab(n)):
            h = head_of_slab(n, w)
            o_refs[mine.index(a // 2)][
                (a % 2) * HALF : (a % 2 + 1) * HALF, h * HD : (h + 1) * HD
            ] = out[w * HALF : (w + 1) * HALF]
    low_half = lax.broadcasted_iota(jnp.int32, (8, HD), 1) < HALF

    def piece(n, v):
        return jnp.broadcast_to(levels[n][:, v * HD : (v + 1) * HD], (8, HD))

    for y in mine:
        rows = []
        for h in range(HEADS - 1):
            one, two = piece(2 * y, h // 2), piece(2 * y + 1, h // 2)
            if h % 2:
                one = pltpu.roll(one, HALF, 1)
            else:
                two = pltpu.roll(two, HALF, 1)
            rows.append(jnp.where(low_half, one, two))
        rows.append(piece(QRUNS + y // 2, y % 2))
        level = jnp.concatenate(rows, axis=1)[:1]
        high = level.astype(jnp.bfloat16).astype(jnp.float32)
        middle = (level - high).astype(jnp.bfloat16).astype(jnp.float32)
        low = level - high - middle
        note = jnp.concatenate(
            [high, middle, low, jnp.zeros((NOTE - 3, HEADS * HD), jnp.float32)], axis=0
        )
        o_refs[mine.index(y)][LOCAL:, :] = note.astype(jnp.bfloat16)


def attend(queries, blocks, state, name, ys=None, wait=()):
    first = not state
    last = ys is not None
    runs = 2 * sum(b.shape[0] for b in blocks)
    smem = pl.BlockSpec(memory_space=pltpu.SMEM)
    vmem = pl.BlockSpec(memory_space=pltpu.VMEM)
    items = SLABS * (runs // BLOCK_RUNS) + 2 * GROUP + 8
    scratch = [
        pltpu.VMEM((runs * HALF, HD), jnp.bfloat16),
        pltpu.VMEM((runs * HALF, HD), jnp.bfloat16),
        pltpu.VMEM((runs // BLOCK_RUNS, ACC_ROWS, BLOCK), jnp.bfloat16),
        pltpu.VMEM((GROUP, BLOCK, COLS), jnp.float32),
        pltpu.VMEM((GROUP, BLOCK, COLS), jnp.float32),
        pltpu.VMEM((HD, HD), jnp.float32),
        pltpu.VMEM((SLABS + 1, 1, COLS), jnp.int32),
        pltpu.VMEM((FACTS, HD), jnp.int32),
        pltpu.SMEM((FACTS, HD), jnp.int32),
        pltpu.SMEM((runs,), jnp.int32),
        pltpu.SMEM((items,), jnp.int32),
        pltpu.SMEM((items,), jnp.int32),
        pltpu.SemaphoreType.DMA(()),
    ]
    seen = jax.ShapeDtypeStruct((QRUNS,), jnp.int32)
    if last:
        one = jax.ShapeDtypeStruct((LOCAL + NOTE, HEADS * HD), jnp.bfloat16)
        out_shape = (one,) * len(ys)
        out_specs = (vmem,) * len(ys)
        scratch = [pltpu.VMEM(s.shape, s.dtype) for s in STATE[2:]] + scratch
    else:
        out_shape = (seen,) + (STATE if first else STATE[2:])
        out_specs = (smem,) + (vmem,) * (len(out_shape) - 1)
    pairs = QRUNS * HEADS * HALF * runs * HALF // 2
    got = pl.pallas_call(
        functools.partial(attend_kernel, first, ys, len(blocks), len(wait)),
        out_shape=out_shape,
        in_specs=([vmem] * len(queries) if first else [])
        + [vmem] * len(blocks)
        + ([] if first else [smem] + [vmem] * len(STATE))
        + [pl.BlockSpec(memory_space=pl.ANY)] * len(wait),
        out_specs=out_specs,
        scratch_shapes=scratch,
        compiler_params=pltpu.CompilerParams(vmem_limit_bytes=20 * 1024 * 1024),
        cost_estimate=pl.CostEstimate(
            flops=4 * pairs * HD, bytes_accessed=runs * HALF * HD * 4, transcendentals=pairs
        ),
        name=name,
    )(*(queries if first else []), *blocks, *state, *wait)
    if last:
        return got
    return got if first else (got[0],) + state[1:3] + got[1:]


def combine_kernel(*refs):
    *o_refs, out_ref = refs
    levels = []
    for o_ref in o_refs:
        note = o_ref[LOCAL:, :].astype(jnp.float32)
        row = note[0:1] + note[1:2] + note[2:3]
        heads = [row[:, h * HD : (h + 1) * HD] for h in range(HEADS)]
        levels.append(
            jnp.concatenate(heads + [jnp.zeros((8 - HEADS, HD), jnp.float32)], axis=0)
        )
    top = functools.reduce(jnp.maximum, levels)
    weights = [jnp.exp2(level - top) for level in levels]
    total = functools.reduce(jnp.add, weights)
    columns = [jnp.transpose(w / total) for w in weights]
    for h in range(HEADS):
        at = slice(h * HD, (h + 1) * HD)
        terms = [
            o_ref[:LOCAL, at].astype(jnp.float32) * column[:, h : h + 1]
            for o_ref, column in zip(o_refs, columns)
        ]
        out_ref[:, at] = functools.reduce(jnp.add, terms).astype(jnp.bfloat16)


def combine(parts):
    vmem = pl.BlockSpec(memory_space=pltpu.VMEM)
    return pl.pallas_call(
        combine_kernel,
        out_shape=jax.ShapeDtypeStruct((LOCAL, HEADS * HD), jnp.bfloat16),
        in_specs=[vmem] * len(parts),
        out_specs=vmem,
        compiler_params=pltpu.CompilerParams(vmem_limit_bytes=8 * 1024 * 1024),
        name="combine",
    )(*parts)


def shift(x, axis, n, by):
    return lax.ppermute(x, axis, [(i, (i + by) % n) for i in range(n)])


def after(arrays, tokens):
    arrays, tokens = list(arrays), list(tokens)

    def nothing(*refs):
        del refs

    whole = pl.BlockSpec(memory_space=pl.ANY)
    got = pl.pallas_call(
        nothing,
        out_shape=[jax.ShapeDtypeStruct(x.shape, x.dtype) for x in arrays],
        in_specs=[whole] * (len(tokens) + len(arrays)),
        out_specs=[whole] * len(arrays),
        input_output_aliases={len(tokens) + i: i for i in range(len(arrays))},
        compiler_params=pltpu.CompilerParams(vmem_limit_bytes=1024 * 1024),
        name="after",
    )(*tokens, *arrays)
    return list(got)


def pack_kernel(place_hbm, q_hbm, k_hbm, v_hbm, kv_out, q_out, place_ref, kv_ref, q_ref, sems):
    copies = [
        pltpu.make_async_copy(place_hbm, place_ref, sems.at[0]),
        pltpu.make_async_copy(k_hbm, kv_ref.at[0], sems.at[1]),
        pltpu.make_async_copy(v_hbm, kv_ref.at[1], sems.at[2]),
        pltpu.make_async_copy(q_hbm, q_ref, sems.at[3]),
    ]
    for copy in copies:
        copy.start()
    for copy in copies:
        copy.wait()
    numbers = [lax.div(place_ref[r * HALF], HALF) for r in range(2)]
    digits = [d for n in numbers for d in (lax.div(n, 16), lax.rem(n, 16))]

    def note(width):
        row = lax.broadcasted_iota(jnp.int32, (NOTE, width), 0)
        got = jnp.zeros((NOTE, width), jnp.int32)
        for i, digit in enumerate(digits):
            got = jnp.where(row == i, digit, got)
        return got.astype(jnp.float32).astype(jnp.bfloat16)

    for i in range(kv_out.shape[0]):
        kv_out[i, :LOCAL, :] = kv_ref[0]
        kv_out[i, LOCAL : 2 * LOCAL, :] = kv_ref[1]
        kv_out[i, 2 * LOCAL :, :] = note(HD)
    q_out[:LOCAL, :] = q_ref[...]
    q_out[LOCAL:, :] = note(HEADS * HD)


def pack(positions, queries, keys, values):
    vmem = pl.BlockSpec(memory_space=pltpu.VMEM)
    return pl.pallas_call(
        pack_kernel,
        out_shape=(
            jax.ShapeDtypeStruct((8, 2 * LOCAL + NOTE, HD), jnp.bfloat16),
            jax.ShapeDtypeStruct((LOCAL + NOTE, HEADS * HD), jnp.bfloat16),
        ),
        in_specs=[pl.BlockSpec(memory_space=pl.ANY)] * 4,
        out_specs=(vmem, vmem),
        scratch_shapes=[
            pltpu.SMEM((LOCAL,), jnp.int32),
            pltpu.VMEM((2, LOCAL, HD), jnp.bfloat16),
            pltpu.VMEM((LOCAL, HEADS * HD), jnp.bfloat16),
            pltpu.SemaphoreType.DMA((4,)),
        ],
        compiler_params=pltpu.CompilerParams(vmem_limit_bytes=56 * 1024 * 1024),
        name="pack",
    )(positions, queries, keys, values)


def halves_kernel(up_ref, down_ref, up_out, down_out):
    up_out[...] = up_ref[: up_out.shape[0]]
    down_out[...] = down_ref[down_out.shape[0] :]


def halves(up, down):
    vmem = pl.BlockSpec(memory_space=pltpu.VMEM)
    half = jax.ShapeDtypeStruct((up.shape[0] // 2,) + up.shape[1:], up.dtype)
    return pl.pallas_call(
        halves_kernel,
        out_shape=(half, half),
        in_specs=[vmem, vmem],
        out_specs=(vmem, vmem),
        compiler_params=pltpu.CompilerParams(vmem_limit_bytes=1024 * 1024),
        name="halves",
    )(up, down)


def local(query_rows, key_rows, value_rows, positions):
    kv, qn = pack(positions, query_rows, key_rows, value_rows)

    def swap(blocks):
        return [shift(b, "c", 2, 1) for b in blocks]

    def pass_on(up, down):
        ring = (0, 2, 1, 3)
        step = [(ring[x], ring[(x + 1) % 4]) for x in range(4)]
        back = [(b, a) for a, b in step]
        return [lax.ppermute(up, ("xl", "xh"), step), lax.ppermute(down, ("xl", "xh"), back)]

    own = lax.all_to_all(kv, "z", 0, 0)
    q1, q2, q3 = (shift(qn, "y", 4, k) for k in (1, 2, 3))
    queries = [q1, q3, q2, qn]
    (own,) = after([own], [q1, q2, q3])
    one = pass_on(own, own)
    own_c = swap([own])
    state = attend(queries, [own] + own_c, (), "attend_0")
    one = after(one, [state[0]])
    two = pass_on(*halves(*one))
    one_c = swap(one)
    state = attend(queries, one + one_c, state, "attend_1")
    two = after(two, [state[0]])
    rest = two + swap(two)
    o1, o3 = attend(queries, rest, state, "attend_2", ys=(0, 1))
    r1, r3 = shift(o1, "y", 4, -1), shift(o3, "y", 4, 1)
    o2, o0 = attend(queries, rest, state, "attend_3", ys=(2, 3), wait=[o1])
    (o2,) = after([o2], [r1, r3])
    return combine([o0, r1, shift(o2, "y", 4, -2), r3])


def solution(mesh):
    fine = Mesh(mesh.devices.reshape(2, 2, 8, 4, 2), AXES)
    rows = P(AXES, None)
    return jax.shard_map(
        local, mesh=fine, in_specs=(rows, rows, rows, P(AXES)), out_specs=rows, check_vma=False
    )
```

```python
import functools
import math

import jax
import jax.numpy as jnp
from jax import lax
from jax.experimental import pallas as pl
from jax.experimental.pallas import tpu as pltpu
from jax.sharding import Mesh, PartitionSpec as P

HD = 128
HEADS = 5
HALF = 64
LOCAL = 128
QRUNS = 8
BLOCK_RUNS = 4
BLOCK = BLOCK_RUNS * HALF
COLS = 4 * HALF
SLABS = QRUNS * HEADS * HALF // COLS
ACC_ROWS = HD + 16
GROUP = 8
NOTE = 16
FACTS = 32
SCALE2 = math.log2(math.e) / math.sqrt(HD)
NEVER = -1e30
SHUT = 1e30
SUM_LIMIT = 1e36

AXES = ("xl", "c", "z", "y", "xh")
STATE = (
    jax.ShapeDtypeStruct((QRUNS, HD), jnp.float32),
    jax.ShapeDtypeStruct((SLABS + 1, HD, COLS), jnp.bfloat16),
    jax.ShapeDtypeStruct((SLABS + 1, ACC_ROWS, COLS), jnp.float32),
    jax.ShapeDtypeStruct((SLABS + 1, 1, COLS), jnp.float32),
)


def runs_of_slab(n):
    return [n] * 4 if n < QRUNS else [(n - QRUNS) * 4 + w for w in range(4)]


def head_of_slab(n, w):
    return w if n < QRUNS else HEADS - 1


def attend_kernel(first, ys, n_kv, n_wait, *refs):
    refs = list(refs)
    last = ys is not None
    mine = list(ys) if last else list(range(QRUNS // 2))
    my_runs = [2 * y + r for y in mine for r in range(2)]
    my_slabs = [n for n in range(SLABS) if set(runs_of_slab(n)) & set(my_runs)]

    def take(n):
        got = refs[:n]
        del refs[:n]
        return got

    if first:
        q_refs = take(QRUNS // 2)
    kv_refs = take(n_kv)
    if not first:
        seen_ref, qnum_in, qt, accs_in, ms_in = take(5)
    take(n_wait)
    if last:
        o_refs = take(len(mine))
    else:
        (o_ref,) = take(1)
    if first:
        qnum, qt, accs, ms = take(4)
    elif last:
        accs, ms = take(2)
    else:
        accs, ms = take(2)
    ks, vs, vt, s0, s1, places, qrun, facts_v, facts, ps, item_slab, item_block, facts_sem = refs
    runs = 2 * sum(ref.shape[0] for ref in kv_refs)
    blocks = runs // BLOCK_RUNS

    def numbers(note):
        note = note.astype(jnp.float32)
        return note[0:1] * 16 + note[1:2], note[2:3] * 16 + note[3:4]

    i = 0
    for ref in kv_refs:
        for g in range(ref.shape[0]):
            one, two = numbers(ref[g, 2 * LOCAL :, :])
            places[i : i + 1, :] = one
            places[i + 1 : i + 2, :] = two
            i += 2
    places[runs:, :] = jnp.full((places.shape[0] - runs, HD), 1e6, jnp.float32)
    down = places[...]
    across = jnp.transpose(down)
    if first:
        q_rows = [n for ref in q_refs for n in numbers(ref[LOCAL:, :HD])]
        qnum[...] = jnp.concatenate(q_rows, axis=0)
    else:
        q_rows = [qnum_in[a : a + 1, :] for a in range(QRUNS)]

    def count(holds):
        return jnp.sum(jnp.where(holds, 1.0, 0.0), axis=0, keepdims=True)

    facts_v[...] = jnp.concatenate(
        [count(down < across), across[0:1]]
        + q_rows
        + [count(down < q) for q in q_rows]
        + [count(down <= q) for q in q_rows]
        + [jnp.zeros((FACTS - 2 - 3 * QRUNS, HD), jnp.float32)],
        axis=0,
    ).astype(jnp.int32)
    copy = pltpu.make_async_copy(facts_v, facts, facts_sem)
    copy.start()

    group = lax.broadcasted_iota(jnp.int32, (1, HD), 1) // HALF
    for n in range(SLABS):
        of = runs_of_slab(n)
        halves = [jnp.where(group == 0, q_rows[of[v]], q_rows[of[v + 1]]) for v in (0, 2)]
        qrun[n] = jnp.concatenate(halves, axis=1).astype(jnp.int32)
    qrun[SLABS] = jnp.zeros((1, COLS), jnp.int32)
    inside = lax.rem(lax.broadcasted_iota(jnp.int32, (1, COLS), 1), HALF)

    if first:
        for n in range(SLABS):
            rows = []
            for w, a in enumerate(runs_of_slab(n)):
                h = head_of_slab(n, w)
                rows.append(
                    q_refs[a // 2][(a % 2) * HALF : (a % 2 + 1) * HALF, h * HD : (h + 1) * HD]
                )
            slab = jnp.concatenate(rows, axis=0).astype(jnp.float32)
            qt[n] = jnp.transpose(slab).astype(jnp.bfloat16)
        qt[SLABS] = jnp.zeros((HD, COLS), jnp.bfloat16)

    def load_state():
        if first:
            accs[...] = jnp.zeros_like(accs)
            ms[...] = jnp.full_like(ms, NEVER)
        else:
            for n in my_slabs:
                accs[n] = accs_in[n]
                ms[n] = ms_in[n]
            accs[SLABS] = jnp.zeros((ACC_ROWS, COLS), jnp.float32)
        ms[SLABS] = jnp.zeros((1, COLS), jnp.float32)

    load_state()
    copy.wait()

    class Column:
        def __init__(self, start):
            self.start = start

        def __getitem__(self, a):
            return facts[self.start + a, 0]

    below, upto = Column(2 + QRUNS), Column(2 + 2 * QRUNS)

    i = 0
    for ref in kv_refs:
        for g in range(ref.shape[0]):
            for r in range(2):
                rank = facts[0, i]
                at = pl.ds(pl.multiple_of(rank * HALF, HALF), HALF)
                ks[at, :] = ref[g, r * HALF : (r + 1) * HALF, :]
                vs[at, :] = ref[g, LOCAL + r * HALF : LOCAL + (r + 1) * HALF, :]
                ps[rank] = facts[1, i]
                i += 1
    for b in range(blocks):
        turned = jnp.transpose(vs[b * BLOCK : (b + 1) * BLOCK, :].astype(jnp.float32))
        vt[b, :HD, :] = turned.astype(jnp.bfloat16)
        vt[b, HD:, :] = jnp.ones((ACC_ROWS - HD, BLOCK), jnp.bfloat16)

    down_run = lax.broadcasted_iota(jnp.int32, (HALF, COLS), 0)

    def first_shift():
        for n in my_slabs:
            s = jnp.dot(ks[:HALF, :], qt[n], preferred_element_type=jnp.float32) * SCALE2
            ok = down_run <= (qrun[n] - ps[0]) * HALF + inside
            top = jnp.max(jnp.where(ok, s, NEVER), axis=0, keepdims=True)
            ms[n] = top if first else jnp.where(ms[n] > 0.5 * NEVER, ms[n], top)

    if first:
        first_shift()
    else:
        fewest = functools.reduce(jnp.minimum, [seen_ref[a] for a in range(QRUNS)])
        pl.when(fewest == 0)(first_shift)

    count = 0
    for n in my_slabs:

        def add(b, k, n=n):
            item_slab[k] = n
            item_block[k] = b
            return k + 1

        end = functools.reduce(jnp.maximum, [below[a] for a in set(runs_of_slab(n))])
        count = lax.fori_loop(0, pl.cdiv(end, BLOCK_RUNS), add, count)
    for e in range(2 * GROUP):
        item_slab[count + e] = SLABS
        item_block[count + e] = 0

    def score(n, b):
        at = pl.ds(pl.multiple_of(b * BLOCK, BLOCK), BLOCK)
        return jnp.dot(ks[at, :], qt[n], preferred_element_type=jnp.float32)

    def consume(s, k):
        n, b = item_slab[k], item_block[k]
        mine, shift = qrun[n], ms[n]
        parts = []
        for t in range(BLOCK_RUNS):
            low = jnp.where(ps[b * BLOCK_RUNS + t] < mine, shift, SHUT)
            p = jnp.exp2(s[t * HALF : (t + 1) * HALF] * SCALE2 - low)
            parts.append(p.astype(jnp.bfloat16))
        p = jnp.concatenate(parts, axis=0)
        accs[n] += jnp.dot(vt[b], p, preferred_element_type=jnp.float32)

    def phase(now, later, base):
        for g in range(GROUP):
            k = base + GROUP + g
            later[g] = score(item_slab[k], item_block[k])
            consume(now[g], base + g)

    @pl.when(count > 0)
    def _():
        for g in range(GROUP):
            s0[g] = score(item_slab[g], item_block[g])
        phases = pl.cdiv(count, GROUP)

        def two(k, c):
            phase(s0, s1, 2 * GROUP * k)
            phase(s1, s0, 2 * GROUP * k + GROUP)
            return c

        lax.fori_loop(0, phases // 2, two, 0)

        @pl.when(lax.rem(phases, 2) == 1)
        def _():
            for g in range(GROUP):
                consume(s0[g], (phases - 1) * GROUP + g)

    def diagonal(a, c):
        @pl.when(upto[a] > below[a])
        def _():
            at = pl.ds(pl.multiple_of(below[a] * HALF, HALF), HALF)
            for n in (a, QRUNS + a // 4):
                s = jnp.dot(ks[at, :], qt[n], preferred_element_type=jnp.float32)
                ok = jnp.logical_and(qrun[n] == facts[2 + a, 0], down_run <= inside)
                p = jnp.where(ok, jnp.exp2(s * SCALE2 - ms[n]), 0.0).astype(jnp.bfloat16)
                accs[n, :HD, :] += lax.dot_general(
                    vs[at, :], p, (((0,), (0,)), ((), ())), preferred_element_type=jnp.float32
                )
                accs[n, HD:, :] += jnp.sum(p.astype(jnp.float32), axis=0, keepdims=True)

        return c

    lax.fori_loop(my_runs[0], my_runs[-1] + 1, diagonal, 0)

    worst = jnp.zeros((1, COLS), jnp.int32)
    for n in my_slabs:
        worst = jnp.maximum(worst, jnp.where(accs[n, HD : HD + 1, :] < SUM_LIMIT, 0, 1))

    @pl.when(jnp.max(worst) > 0)
    def _():
        load_state()

        def per_slab(n, c):
            def online(b, c):
                s = score(n, b) * SCALE2
                keep = jnp.concatenate(
                    [
                        jnp.where(
                            down_run <= (qrun[n] - ps[b * BLOCK_RUNS + t]) * HALF + inside, 0.0, 1.0
                        )
                        for t in range(BLOCK_RUNS)
                    ],
                    axis=0,
                )
                old = ms[n]
                s = jnp.where(keep > 0, NEVER, s)
                new = jnp.maximum(old, jnp.max(s, axis=0, keepdims=True))
                p = jnp.where(keep > 0, 0.0, jnp.exp2(s - new))
                ms[n] = new
                accs[n] = accs[n] * jnp.exp2(old - new) + jnp.dot(
                    vt[b], p.astype(jnp.bfloat16), preferred_element_type=jnp.float32
                )
                return c

            return lax.fori_loop(0, blocks, online, c)

        for n in my_slabs:
            per_slab(n, 0)

    if not last:
        for a in range(QRUNS):
            o_ref[a] = upto[a] if first else seen_ref[a] + upto[a]
        return
    levels = {}
    for n in my_slabs:
        total = accs[n, HD : HD + 1, :]
        some = total > 0
        safe = jnp.where(some, total, 1.0)
        levels[n] = jnp.where(some, ms[n] + jnp.log2(safe), NEVER)
        out = jnp.transpose(accs[n, :HD, :] / safe).astype(jnp.bfloat16)
        for w, a in enumerate(runs_of_slab(n)):
            if a not in my_runs:
                continue
            h = head_of_slab(n, w)
            o_refs[mine.index(a // 2)][
                (a % 2) * HALF : (a % 2 + 1) * HALF, h * HD : (h + 1) * HD
            ] = out[w * HALF : (w + 1) * HALF]
    low_half = lax.broadcasted_iota(jnp.int32, (8, HD), 1) < HALF

    def piece(n, v):
        return jnp.broadcast_to(levels[n][:, v * HD : (v + 1) * HD], (8, HD))

    for y in mine:
        rows = []
        for h in range(HEADS - 1):
            one, two = piece(2 * y, h // 2), piece(2 * y + 1, h // 2)
            if h % 2:
                one = pltpu.roll(one, HALF, 1)
            else:
                two = pltpu.roll(two, HALF, 1)
            rows.append(jnp.where(low_half, one, two))
        rows.append(piece(QRUNS + y // 2, y % 2))
        level = jnp.concatenate(rows, axis=1)[:1]
        high = level.astype(jnp.bfloat16).astype(jnp.float32)
        middle = (level - high).astype(jnp.bfloat16).astype(jnp.float32)
        low = level - high - middle
        note = jnp.concatenate(
            [high, middle, low, jnp.zeros((NOTE - 3, HEADS * HD), jnp.float32)], axis=0
        )
        o_refs[mine.index(y)][LOCAL:, :] = note.astype(jnp.bfloat16)


def attend(queries, blocks, state, name, ys=None, wait=()):
    first = not state
    last = ys is not None
    runs = 2 * sum(b.shape[0] for b in blocks)
    smem = pl.BlockSpec(memory_space=pltpu.SMEM)
    vmem = pl.BlockSpec(memory_space=pltpu.VMEM)
    items = SLABS * (runs // BLOCK_RUNS) + 2 * GROUP + 8
    scratch = [
        pltpu.VMEM((runs * HALF, HD), jnp.bfloat16),
        pltpu.VMEM((runs * HALF, HD), jnp.bfloat16),
        pltpu.VMEM((runs // BLOCK_RUNS, ACC_ROWS, BLOCK), jnp.bfloat16),
        pltpu.VMEM((GROUP, BLOCK, COLS), jnp.float32),
        pltpu.VMEM((GROUP, BLOCK, COLS), jnp.float32),
        pltpu.VMEM((HD, HD), jnp.float32),
        pltpu.VMEM((SLABS + 1, 1, COLS), jnp.int32),
        pltpu.VMEM((FACTS, HD), jnp.int32),
        pltpu.SMEM((FACTS, HD), jnp.int32),
        pltpu.SMEM((runs,), jnp.int32),
        pltpu.SMEM((items,), jnp.int32),
        pltpu.SMEM((items,), jnp.int32),
        pltpu.SemaphoreType.DMA(()),
    ]
    seen = jax.ShapeDtypeStruct((QRUNS,), jnp.int32)
    if last:
        one = jax.ShapeDtypeStruct((LOCAL + NOTE, HEADS * HD), jnp.bfloat16)
        out_shape = (one,) * len(ys)
        out_specs = (vmem,) * len(ys)
        scratch = [pltpu.VMEM(s.shape, s.dtype) for s in STATE[2:]] + scratch
    else:
        out_shape = (seen,) + (STATE if first else STATE[2:])
        out_specs = (smem,) + (vmem,) * (len(out_shape) - 1)
    pairs = QRUNS * HEADS * HALF * runs * HALF // 2
    got = pl.pallas_call(
        functools.partial(attend_kernel, first, ys, len(blocks), len(wait)),
        out_shape=out_shape,
        in_specs=([vmem] * len(queries) if first else [])
        + [vmem] * len(blocks)
        + ([] if first else [smem] + [vmem] * len(STATE))
        + [pl.BlockSpec(memory_space=pl.ANY)] * len(wait),
        out_specs=out_specs,
        scratch_shapes=scratch,
        compiler_params=pltpu.CompilerParams(vmem_limit_bytes=20 * 1024 * 1024),
        cost_estimate=pl.CostEstimate(
            flops=4 * pairs * HD, bytes_accessed=runs * HALF * HD * 4, transcendentals=pairs
        ),
        name=name,
    )(*(queries if first else []), *blocks, *state, *wait)
    if last:
        return got
    return got if first else (got[0],) + state[1:3] + got[1:]


def combine_kernel(*refs):
    *o_refs, out_ref = refs
    levels = []
    for o_ref in o_refs:
        note = o_ref[LOCAL:, :].astype(jnp.float32)
        row = note[0:1] + note[1:2] + note[2:3]
        heads = [row[:, h * HD : (h + 1) * HD] for h in range(HEADS)]
        levels.append(
            jnp.concatenate(heads + [jnp.zeros((8 - HEADS, HD), jnp.float32)], axis=0)
        )
    top = functools.reduce(jnp.maximum, levels)
    weights = [jnp.exp2(level - top) for level in levels]
    total = functools.reduce(jnp.add, weights)
    columns = [jnp.transpose(w / total) for w in weights]
    for h in range(HEADS):
        at = slice(h * HD, (h + 1) * HD)
        terms = [
            o_ref[:LOCAL, at].astype(jnp.float32) * column[:, h : h + 1]
            for o_ref, column in zip(o_refs, columns)
        ]
        out_ref[:, at] = functools.reduce(jnp.add, terms).astype(jnp.bfloat16)


def combine(parts):
    vmem = pl.BlockSpec(memory_space=pltpu.VMEM)
    return pl.pallas_call(
        combine_kernel,
        out_shape=jax.ShapeDtypeStruct((LOCAL, HEADS * HD), jnp.bfloat16),
        in_specs=[vmem] * len(parts),
        out_specs=vmem,
        compiler_params=pltpu.CompilerParams(vmem_limit_bytes=8 * 1024 * 1024),
        name="combine",
    )(*parts)


def shift(x, axis, n, by):
    return lax.ppermute(x, axis, [(i, (i + by) % n) for i in range(n)])


def after(arrays, tokens):
    arrays, tokens = list(arrays), list(tokens)

    def nothing(*refs):
        del refs

    whole = pl.BlockSpec(memory_space=pl.ANY)
    got = pl.pallas_call(
        nothing,
        out_shape=[jax.ShapeDtypeStruct(x.shape, x.dtype) for x in arrays],
        in_specs=[whole] * (len(tokens) + len(arrays)),
        out_specs=[whole] * len(arrays),
        input_output_aliases={len(tokens) + i: i for i in range(len(arrays))},
        compiler_params=pltpu.CompilerParams(vmem_limit_bytes=1024 * 1024),
        name="after",
    )(*tokens, *arrays)
    return list(got)


def pack_kernel(place_hbm, q_hbm, k_hbm, v_hbm, kv_out, q_out, place_ref, kv_ref, q_ref, sems):
    copies = [
        pltpu.make_async_copy(place_hbm, place_ref, sems.at[0]),
        pltpu.make_async_copy(k_hbm, kv_ref.at[0], sems.at[1]),
        pltpu.make_async_copy(v_hbm, kv_ref.at[1], sems.at[2]),
        pltpu.make_async_copy(q_hbm, q_ref, sems.at[3]),
    ]
    for copy in copies:
        copy.start()
    for copy in copies:
        copy.wait()
    numbers = [lax.div(place_ref[r * HALF], HALF) for r in range(2)]
    digits = [d for n in numbers for d in (lax.div(n, 16), lax.rem(n, 16))]

    def note(width):
        row = lax.broadcasted_iota(jnp.int32, (NOTE, width), 0)
        got = jnp.zeros((NOTE, width), jnp.int32)
        for i, digit in enumerate(digits):
            got = jnp.where(row == i, digit, got)
        return got.astype(jnp.float32).astype(jnp.bfloat16)

    for i in range(kv_out.shape[0]):
        kv_out[i, :LOCAL, :] = kv_ref[0]
        kv_out[i, LOCAL : 2 * LOCAL, :] = kv_ref[1]
        kv_out[i, 2 * LOCAL :, :] = note(HD)
    q_out[:LOCAL, :] = q_ref[...]
    q_out[LOCAL:, :] = note(HEADS * HD)


def pack(positions, queries, keys, values):
    vmem = pl.BlockSpec(memory_space=pltpu.VMEM)
    return pl.pallas_call(
        pack_kernel,
        out_shape=(
            jax.ShapeDtypeStruct((8, 2 * LOCAL + NOTE, HD), jnp.bfloat16),
            jax.ShapeDtypeStruct((LOCAL + NOTE, HEADS * HD), jnp.bfloat16),
        ),
        in_specs=[pl.BlockSpec(memory_space=pl.ANY)] * 4,
        out_specs=(vmem, vmem),
        scratch_shapes=[
            pltpu.SMEM((LOCAL,), jnp.int32),
            pltpu.VMEM((2, LOCAL, HD), jnp.bfloat16),
            pltpu.VMEM((LOCAL, HEADS * HD), jnp.bfloat16),
            pltpu.SemaphoreType.DMA((4,)),
        ],
        compiler_params=pltpu.CompilerParams(vmem_limit_bytes=56 * 1024 * 1024),
        name="pack",
    )(positions, queries, keys, values)


def pick_kernel(plan, n_in, *refs):
    for pieces, out_ref in zip(plan, refs[n_in:]):
        at = 0
        for source, low, high in pieces:
            out_ref[at : at + high - low] = refs[source][low:high]
            at += high - low


def pick(arrays, plan):
    vmem = pl.BlockSpec(memory_space=pltpu.VMEM)
    rows = [sum(high - low for _, low, high in pieces) for pieces in plan]
    return pl.pallas_call(
        functools.partial(pick_kernel, plan, len(arrays)),
        out_shape=[
            jax.ShapeDtypeStruct((n,) + arrays[0].shape[1:], arrays[0].dtype) for n in rows
        ],
        in_specs=[vmem] * len(arrays),
        out_specs=[vmem] * len(plan),
        compiler_params=pltpu.CompilerParams(vmem_limit_bytes=1024 * 1024),
        name="pick",
    )(*arrays)


def local(query_rows, key_rows, value_rows, positions):
    kv, qn = pack(positions, query_rows, key_rows, value_rows)

    def swap(blocks):
        return [shift(b, "c", 2, 1) for b in blocks]

    def pass_on(up, down):
        ring = (0, 2, 1, 3)
        step = [(ring[x], ring[(x + 1) % 4]) for x in range(4)]
        back = [(b, a) for a, b in step]
        return [lax.ppermute(up, ("xl", "xh"), step), lax.ppermute(down, ("xl", "xh"), back)]

    own = lax.all_to_all(kv, "z", 0, 0)
    q1, q2, q3 = (shift(qn, "y", 4, k) for k in (1, 2, 3))
    queries = [q1, q2, q3, qn]
    (own,) = after([own], [q1, q2, q3])
    one = pass_on(*pick([own], [[(0, 0, 6)], [(0, 2, 8)]]))
    own_c = swap([own])
    state = attend(queries, [own] + own_c, (), "attend_0")
    one = after(one, [state[0]])
    two = pass_on(*pick([own, *one], [[(0, 6, 8), (1, 0, 4)], [(0, 0, 2), (2, 2, 6)]]))
    one_c = swap(one)
    state = attend(queries, one + one_c, state, "attend_1")
    two = after(two, [state[0]])
    rest = two + swap(two)
    outs = attend(queries, rest, state, "attend_2", ys=(0, 1, 2))
    (mine,) = attend(queries, rest, state, "attend_3", ys=(3,), wait=outs[:1])
    return combine([mine] + [shift(o, "y", 4, -k) for k, o in zip((1, 2, 3), outs)])


def solution(mesh):
    fine = Mesh(mesh.devices.reshape(2, 2, 8, 4, 2), AXES)
    rows = P(AXES, None)
    return jax.shard_map(
        local, mesh=fine, in_specs=(rows, rows, rows, P(AXES)), out_specs=rows, check_vma=False
    )
```

```python
import functools
import math

import jax
import jax.numpy as jnp
from jax import lax
from jax.experimental import pallas as pl
from jax.experimental.pallas import tpu as pltpu
from jax.sharding import Mesh, PartitionSpec as P

HD = 128
HEADS = 5
HALF = 64
LOCAL = 128
QRUNS = 8
BLOCK_RUNS = 4
BLOCK = BLOCK_RUNS * HALF
COLS = 4 * HALF
SLABS = QRUNS * HEADS * HALF // COLS
ACC_ROWS = HD + 16
GROUP = 8
NOTE = 16
FACTS = 32
SCALE2 = math.log2(math.e) / math.sqrt(HD)
NEVER = -1e30
SHUT = 1e30
SUM_LIMIT = 1e36

AXES = ("xl", "c", "z", "y", "xh")
STATE = (
    jax.ShapeDtypeStruct((QRUNS, HD), jnp.float32),
    jax.ShapeDtypeStruct((SLABS + 1, HD, COLS), jnp.bfloat16),
    jax.ShapeDtypeStruct((SLABS + 1, ACC_ROWS, COLS), jnp.float32),
    jax.ShapeDtypeStruct((SLABS + 1, 1, COLS), jnp.float32),
)


def runs_of_slab(n):
    return [n] * 4 if n < QRUNS else [(n - QRUNS) * 4 + w for w in range(4)]


def head_of_slab(n, w):
    return w if n < QRUNS else HEADS - 1


def attend_kernel(first, ys, n_kv, n_wait, *refs):
    refs = list(refs)
    last = ys is not None
    mine = list(ys) if last else list(range(QRUNS // 2))
    my_runs = [2 * y + r for y in mine for r in range(2)]
    my_slabs = [n for n in range(SLABS) if set(runs_of_slab(n)) & set(my_runs)]

    def take(n):
        got = refs[:n]
        del refs[:n]
        return got

    if first:
        q_refs = take(QRUNS // 2)
    kv_refs = take(n_kv)
    if not first:
        seen_ref, qnum_in, qt, accs_in, ms_in = take(5)
    take(n_wait)
    if last:
        o_refs = take(len(mine))
    else:
        (o_ref,) = take(1)
    if first:
        qnum, qt, accs, ms = take(4)
    elif last:
        accs, ms = take(2)
    else:
        accs, ms = take(2)
    ks, vs, vt, s0, s1, places, qrun, facts_v, facts, ps, item_slab, item_block, facts_sem = refs
    runs = 2 * sum(ref.shape[0] for ref in kv_refs)
    blocks = runs // BLOCK_RUNS

    def numbers(note):
        note = note.astype(jnp.float32)
        return note[0:1] * 16 + note[1:2], note[2:3] * 16 + note[3:4]

    i = 0
    for ref in kv_refs:
        for g in range(ref.shape[0]):
            one, two = numbers(ref[g, 2 * LOCAL :, :])
            places[i : i + 1, :] = one
            places[i + 1 : i + 2, :] = two
            i += 2
    places[runs:, :] = jnp.full((places.shape[0] - runs, HD), 1e6, jnp.float32)
    down = places[...]
    across = jnp.transpose(down)
    if first:
        q_rows = [n for ref in q_refs for n in numbers(ref[LOCAL:, :HD])]
        qnum[...] = jnp.concatenate(q_rows, axis=0)
    else:
        q_rows = [qnum_in[a : a + 1, :] for a in range(QRUNS)]

    def count(holds):
        return jnp.sum(jnp.where(holds, 1.0, 0.0), axis=0, keepdims=True)

    facts_v[...] = jnp.concatenate(
        [count(down < across), across[0:1]]
        + q_rows
        + [count(down < q) for q in q_rows]
        + [count(down <= q) for q in q_rows]
        + [jnp.zeros((FACTS - 2 - 3 * QRUNS, HD), jnp.float32)],
        axis=0,
    ).astype(jnp.int32)
    copy = pltpu.make_async_copy(facts_v, facts, facts_sem)
    copy.start()

    group = lax.broadcasted_iota(jnp.int32, (1, HD), 1) // HALF
    for n in range(SLABS):
        of = runs_of_slab(n)
        halves = [jnp.where(group == 0, q_rows[of[v]], q_rows[of[v + 1]]) for v in (0, 2)]
        qrun[n] = jnp.concatenate(halves, axis=1).astype(jnp.int32)
    qrun[SLABS] = jnp.zeros((1, COLS), jnp.int32)
    inside = lax.rem(lax.broadcasted_iota(jnp.int32, (1, COLS), 1), HALF)

    if first:
        for n in range(SLABS):
            rows = []
            for w, a in enumerate(runs_of_slab(n)):
                h = head_of_slab(n, w)
                rows.append(
                    q_refs[a // 2][(a % 2) * HALF : (a % 2 + 1) * HALF, h * HD : (h + 1) * HD]
                )
            slab = jnp.concatenate(rows, axis=0).astype(jnp.float32)
            qt[n] = jnp.transpose(slab).astype(jnp.bfloat16)
        qt[SLABS] = jnp.zeros((HD, COLS), jnp.bfloat16)

    def load_state():
        if first:
            accs[...] = jnp.zeros_like(accs)
            ms[...] = jnp.full_like(ms, NEVER)
        else:
            for n in my_slabs:
                accs[n] = accs_in[n]
                ms[n] = ms_in[n]
            accs[SLABS] = jnp.zeros((ACC_ROWS, COLS), jnp.float32)
        ms[SLABS] = jnp.zeros((1, COLS), jnp.float32)

    load_state()
    copy.wait()

    class Column:
        def __init__(self, start):
            self.start = start

        def __getitem__(self, a):
            return facts[self.start + a, 0]

    below, upto = Column(2 + QRUNS), Column(2 + 2 * QRUNS)

    i = 0
    for ref in kv_refs:
        for g in range(ref.shape[0]):
            for r in range(2):
                rank = facts[0, i]
                at = pl.ds(pl.multiple_of(rank * HALF, HALF), HALF)
                ks[at, :] = ref[g, r * HALF : (r + 1) * HALF, :]
                vs[at, :] = ref[g, LOCAL + r * HALF : LOCAL + (r + 1) * HALF, :]
                ps[rank] = facts[1, i]
                i += 1
    for b in range(blocks):
        turned = jnp.transpose(vs[b * BLOCK : (b + 1) * BLOCK, :].astype(jnp.float32))
        vt[b, :HD, :] = turned.astype(jnp.bfloat16)
        vt[b, HD:, :] = jnp.ones((ACC_ROWS - HD, BLOCK), jnp.bfloat16)

    down_run = lax.broadcasted_iota(jnp.int32, (HALF, COLS), 0)

    def first_shift():
        for n in my_slabs:
            s = jnp.dot(ks[:HALF, :], qt[n], preferred_element_type=jnp.float32) * SCALE2
            ok = down_run <= (qrun[n] - ps[0]) * HALF + inside
            top = jnp.max(jnp.where(ok, s, NEVER), axis=0, keepdims=True)
            ms[n] = top if first else jnp.where(ms[n] > 0.5 * NEVER, ms[n], top)

    if first:
        first_shift()
    else:
        fewest = functools.reduce(jnp.minimum, [seen_ref[a] for a in range(QRUNS)])
        pl.when(fewest == 0)(first_shift)

    count = 0
    for n in my_slabs:

        def add(b, k, n=n):
            item_slab[k] = n
            item_block[k] = b
            return k + 1

        end = functools.reduce(jnp.maximum, [below[a] for a in set(runs_of_slab(n))])
        count = lax.fori_loop(0, pl.cdiv(end, BLOCK_RUNS), add, count)
    for e in range(2 * GROUP):
        item_slab[count + e] = SLABS
        item_block[count + e] = 0

    def score(n, b):
        at = pl.ds(pl.multiple_of(b * BLOCK, BLOCK), BLOCK)
        return jnp.dot(ks[at, :], qt[n], preferred_element_type=jnp.float32)

    def consume(s, k):
        n, b = item_slab[k], item_block[k]
        mine, shift = qrun[n], ms[n]
        parts = []
        for t in range(BLOCK_RUNS):
            low = jnp.where(ps[b * BLOCK_RUNS + t] < mine, shift, SHUT)
            p = jnp.exp2(s[t * HALF : (t + 1) * HALF] * SCALE2 - low)
            parts.append(p.astype(jnp.bfloat16))
        p = jnp.concatenate(parts, axis=0)
        accs[n] += jnp.dot(vt[b], p, preferred_element_type=jnp.float32)

    def phase(now, later, base):
        for g in range(GROUP):
            k = base + GROUP + g
            later[g] = score(item_slab[k], item_block[k])
            consume(now[g], base + g)

    @pl.when(count > 0)
    def _():
        for g in range(GROUP):
            s0[g] = score(item_slab[g], item_block[g])
        phases = pl.cdiv(count, GROUP)

        def two(k, c):
            phase(s0, s1, 2 * GROUP * k)
            phase(s1, s0, 2 * GROUP * k + GROUP)
            return c

        lax.fori_loop(0, phases // 2, two, 0)

        @pl.when(lax.rem(phases, 2) == 1)
        def _():
            for g in range(GROUP):
                consume(s0[g], (phases - 1) * GROUP + g)

    def diagonal(a, c):
        @pl.when(upto[a] > below[a])
        def _():
            at = pl.ds(pl.multiple_of(below[a] * HALF, HALF), HALF)
            for n in (a, QRUNS + a // 4):
                s = jnp.dot(ks[at, :], qt[n], preferred_element_type=jnp.float32)
                ok = jnp.logical_and(qrun[n] == facts[2 + a, 0], down_run <= inside)
                p = jnp.where(ok, jnp.exp2(s * SCALE2 - ms[n]), 0.0).astype(jnp.bfloat16)
                accs[n, :HD, :] += lax.dot_general(
                    vs[at, :], p, (((0,), (0,)), ((), ())), preferred_element_type=jnp.float32
                )
                accs[n, HD:, :] += jnp.sum(p.astype(jnp.float32), axis=0, keepdims=True)

        return c

    lax.fori_loop(my_runs[0], my_runs[-1] + 1, diagonal, 0)

    worst = jnp.zeros((1, COLS), jnp.int32)
    for n in my_slabs:
        worst = jnp.maximum(worst, jnp.where(accs[n, HD : HD + 1, :] < SUM_LIMIT, 0, 1))

    @pl.when(jnp.max(worst) > 0)
    def _():
        load_state()

        def per_slab(n, c):
            def online(b, c):
                s = score(n, b) * SCALE2
                keep = jnp.concatenate(
                    [
                        jnp.where(
                            down_run <= (qrun[n] - ps[b * BLOCK_RUNS + t]) * HALF + inside, 0.0, 1.0
                        )
                        for t in range(BLOCK_RUNS)
                    ],
                    axis=0,
                )
                old = ms[n]
                s = jnp.where(keep > 0, NEVER, s)
                new = jnp.maximum(old, jnp.max(s, axis=0, keepdims=True))
                p = jnp.where(keep > 0, 0.0, jnp.exp2(s - new))
                ms[n] = new
                accs[n] = accs[n] * jnp.exp2(old - new) + jnp.dot(
                    vt[b], p.astype(jnp.bfloat16), preferred_element_type=jnp.float32
                )
                return c

            return lax.fori_loop(0, blocks, online, c)

        for n in my_slabs:
            per_slab(n, 0)

    if not last:
        for a in range(QRUNS):
            o_ref[a] = upto[a] if first else seen_ref[a] + upto[a]
        return
    levels = {}
    for n in my_slabs:
        total = accs[n, HD : HD + 1, :]
        some = total > 0
        safe = jnp.where(some, total, 1.0)
        levels[n] = jnp.where(some, ms[n] + jnp.log2(safe), NEVER)
        out = jnp.transpose(accs[n, :HD, :] / safe).astype(jnp.bfloat16)
        for w, a in enumerate(runs_of_slab(n)):
            if a not in my_runs:
                continue
            h = head_of_slab(n, w)
            o_refs[mine.index(a // 2)][
                (a % 2) * HALF : (a % 2 + 1) * HALF, h * HD : (h + 1) * HD
            ] = out[w * HALF : (w + 1) * HALF]
    low_half = lax.broadcasted_iota(jnp.int32, (8, HD), 1) < HALF

    def piece(n, v):
        return jnp.broadcast_to(levels[n][:, v * HD : (v + 1) * HD], (8, HD))

    for y in mine:
        rows = []
        for h in range(HEADS - 1):
            one, two = piece(2 * y, h // 2), piece(2 * y + 1, h // 2)
            if h % 2:
                one = pltpu.roll(one, HALF, 1)
            else:
                two = pltpu.roll(two, HALF, 1)
            rows.append(jnp.where(low_half, one, two))
        rows.append(piece(QRUNS + y // 2, y % 2))
        level = jnp.concatenate(rows, axis=1)[:1]
        high = level.astype(jnp.bfloat16).astype(jnp.float32)
        middle = (level - high).astype(jnp.bfloat16).astype(jnp.float32)
        low = level - high - middle
        note = jnp.concatenate(
            [high, middle, low, jnp.zeros((NOTE - 3, HEADS * HD), jnp.float32)], axis=0
        )
        o_refs[mine.index(y)][LOCAL:, :] = note.astype(jnp.bfloat16)


def attend(queries, blocks, state, name, ys=None, wait=()):
    first = not state
    last = ys is not None
    runs = 2 * sum(b.shape[0] for b in blocks)
    smem = pl.BlockSpec(memory_space=pltpu.SMEM)
    vmem = pl.BlockSpec(memory_space=pltpu.VMEM)
    items = SLABS * (runs // BLOCK_RUNS) + 2 * GROUP + 8
    scratch = [
        pltpu.VMEM((runs * HALF, HD), jnp.bfloat16),
        pltpu.VMEM((runs * HALF, HD), jnp.bfloat16),
        pltpu.VMEM((runs // BLOCK_RUNS, ACC_ROWS, BLOCK), jnp.bfloat16),
        pltpu.VMEM((GROUP, BLOCK, COLS), jnp.float32),
        pltpu.VMEM((GROUP, BLOCK, COLS), jnp.float32),
        pltpu.VMEM((HD, HD), jnp.float32),
        pltpu.VMEM((SLABS + 1, 1, COLS), jnp.int32),
        pltpu.VMEM((FACTS, HD), jnp.int32),
        pltpu.SMEM((FACTS, HD), jnp.int32),
        pltpu.SMEM((runs,), jnp.int32),
        pltpu.SMEM((items,), jnp.int32),
        pltpu.SMEM((items,), jnp.int32),
        pltpu.SemaphoreType.DMA(()),
    ]
    seen = jax.ShapeDtypeStruct((QRUNS,), jnp.int32)
    if last:
        one = jax.ShapeDtypeStruct((LOCAL + NOTE, HEADS * HD), jnp.bfloat16)
        out_shape = (one,) * len(ys)
        out_specs = (vmem,) * len(ys)
        scratch = [pltpu.VMEM(s.shape, s.dtype) for s in STATE[2:]] + scratch
    else:
        out_shape = (seen,) + (STATE if first else STATE[2:])
        out_specs = (smem,) + (vmem,) * (len(out_shape) - 1)
    pairs = QRUNS * HEADS * HALF * runs * HALF // 2
    got = pl.pallas_call(
        functools.partial(attend_kernel, first, ys, len(blocks), len(wait)),
        out_shape=out_shape,
        in_specs=([vmem] * len(queries) if first else [])
        + [vmem] * len(blocks)
        + ([] if first else [smem] + [vmem] * len(STATE))
        + [pl.BlockSpec(memory_space=pl.ANY)] * len(wait),
        out_specs=out_specs,
        scratch_shapes=scratch,
        compiler_params=pltpu.CompilerParams(vmem_limit_bytes=20 * 1024 * 1024),
        cost_estimate=pl.CostEstimate(
            flops=4 * pairs * HD, bytes_accessed=runs * HALF * HD * 4, transcendentals=pairs
        ),
        name=name,
    )(*(queries if first else []), *blocks, *state, *wait)
    if last:
        return got
    return got if first else (got[0],) + state[1:3] + got[1:]


def combine_kernel(*refs):
    *o_refs, out_ref = refs
    levels = []
    for o_ref in o_refs:
        note = o_ref[LOCAL:, :].astype(jnp.float32)
        row = note[0:1] + note[1:2] + note[2:3]
        heads = [row[:, h * HD : (h + 1) * HD] for h in range(HEADS)]
        levels.append(
            jnp.concatenate(heads + [jnp.zeros((8 - HEADS, HD), jnp.float32)], axis=0)
        )
    top = functools.reduce(jnp.maximum, levels)
    weights = [jnp.exp2(level - top) for level in levels]
    total = functools.reduce(jnp.add, weights)
    columns = [jnp.transpose(w / total) for w in weights]
    for h in range(HEADS):
        at = slice(h * HD, (h + 1) * HD)
        terms = [
            o_ref[:LOCAL, at].astype(jnp.float32) * column[:, h : h + 1]
            for o_ref, column in zip(o_refs, columns)
        ]
        out_ref[:, at] = functools.reduce(jnp.add, terms).astype(jnp.bfloat16)


def combine(parts):
    vmem = pl.BlockSpec(memory_space=pltpu.VMEM)
    return pl.pallas_call(
        combine_kernel,
        out_shape=jax.ShapeDtypeStruct((LOCAL, HEADS * HD), jnp.bfloat16),
        in_specs=[vmem] * len(parts),
        out_specs=vmem,
        compiler_params=pltpu.CompilerParams(vmem_limit_bytes=8 * 1024 * 1024),
        name="combine",
    )(*parts)


def shift(x, axis, n, by):
    return lax.ppermute(x, axis, [(i, (i + by) % n) for i in range(n)])


def after(arrays, tokens):
    arrays, tokens = list(arrays), list(tokens)

    def nothing(*refs):
        del refs

    whole = pl.BlockSpec(memory_space=pl.ANY)
    got = pl.pallas_call(
        nothing,
        out_shape=[jax.ShapeDtypeStruct(x.shape, x.dtype) for x in arrays],
        in_specs=[whole] * (len(tokens) + len(arrays)),
        out_specs=[whole] * len(arrays),
        input_output_aliases={len(tokens) + i: i for i in range(len(arrays))},
        compiler_params=pltpu.CompilerParams(vmem_limit_bytes=1024 * 1024),
        name="after",
    )(*tokens, *arrays)
    return list(got)


def pack_kernel(place_hbm, q_hbm, k_hbm, v_hbm, kv_out, q_out, place_ref, kv_ref, q_ref, sems):
    copies = [
        pltpu.make_async_copy(place_hbm, place_ref, sems.at[0]),
        pltpu.make_async_copy(k_hbm, kv_ref.at[0], sems.at[1]),
        pltpu.make_async_copy(v_hbm, kv_ref.at[1], sems.at[2]),
        pltpu.make_async_copy(q_hbm, q_ref, sems.at[3]),
    ]
    for copy in copies:
        copy.start()
    for copy in copies:
        copy.wait()
    numbers = [lax.div(place_ref[r * HALF], HALF) for r in range(2)]
    digits = [d for n in numbers for d in (lax.div(n, 16), lax.rem(n, 16))]

    def note(width):
        row = lax.broadcasted_iota(jnp.int32, (NOTE, width), 0)
        got = jnp.zeros((NOTE, width), jnp.int32)
        for i, digit in enumerate(digits):
            got = jnp.where(row == i, digit, got)
        return got.astype(jnp.float32).astype(jnp.bfloat16)

    for i in range(kv_out.shape[0]):
        kv_out[i, :LOCAL, :] = kv_ref[0]
        kv_out[i, LOCAL : 2 * LOCAL, :] = kv_ref[1]
        kv_out[i, 2 * LOCAL :, :] = note(HD)
    q_out[:LOCAL, :] = q_ref[...]
    q_out[LOCAL:, :] = note(HEADS * HD)


def pack(positions, queries, keys, values):
    vmem = pl.BlockSpec(memory_space=pltpu.VMEM)
    return pl.pallas_call(
        pack_kernel,
        out_shape=(
            jax.ShapeDtypeStruct((8, 2 * LOCAL + NOTE, HD), jnp.bfloat16),
            jax.ShapeDtypeStruct((LOCAL + NOTE, HEADS * HD), jnp.bfloat16),
        ),
        in_specs=[pl.BlockSpec(memory_space=pl.ANY)] * 4,
        out_specs=(vmem, vmem),
        scratch_shapes=[
            pltpu.SMEM((LOCAL,), jnp.int32),
            pltpu.VMEM((2, LOCAL, HD), jnp.bfloat16),
            pltpu.VMEM((LOCAL, HEADS * HD), jnp.bfloat16),
            pltpu.SemaphoreType.DMA((4,)),
        ],
        compiler_params=pltpu.CompilerParams(vmem_limit_bytes=56 * 1024 * 1024),
        name="pack",
    )(positions, queries, keys, values)


def pick_kernel(plan, n_in, *refs):
    for pieces, out_ref in zip(plan, refs[n_in:]):
        at = 0
        for source, low, high in pieces:
            out_ref[at : at + high - low] = refs[source][low:high]
            at += high - low


def pick(arrays, plan):
    vmem = pl.BlockSpec(memory_space=pltpu.VMEM)
    rows = [sum(high - low for _, low, high in pieces) for pieces in plan]
    return pl.pallas_call(
        functools.partial(pick_kernel, plan, len(arrays)),
        out_shape=[
            jax.ShapeDtypeStruct((n,) + arrays[0].shape[1:], arrays[0].dtype) for n in rows
        ],
        in_specs=[vmem] * len(arrays),
        out_specs=[vmem] * len(plan),
        compiler_params=pltpu.CompilerParams(vmem_limit_bytes=1024 * 1024),
        name="pick",
    )(*arrays)


def local(query_rows, key_rows, value_rows, positions):
    kv, qn = pack(positions, query_rows, key_rows, value_rows)

    def swap(blocks):
        return [shift(b, "c", 2, 1) for b in blocks]

    def pass_on(up, down):
        ring = (0, 2, 1, 3)
        step = [(ring[x], ring[(x + 1) % 4]) for x in range(4)]
        back = [(b, a) for a, b in step]
        return [lax.ppermute(up, ("xl", "xh"), step), lax.ppermute(down, ("xl", "xh"), back)]

    own = lax.all_to_all(kv, "z", 0, 0)
    q2, q1, q3 = (shift(qn, "y", 4, k) for k in (2, 1, 3))
    queries = [q1, q2, q3, qn]
    (own,) = after([own], [q2, q1, q3])
    one = pass_on(*pick([own], [[(0, 0, 6)], [(0, 2, 8)]]))
    own_c = swap([own])
    state = attend(queries, [own] + own_c, (), "attend_0")
    one = after(one, [state[0]])
    two = pass_on(*pick([own, *one], [[(0, 6, 8), (1, 0, 4)], [(0, 0, 2), (2, 2, 6)]]))
    one_c = swap(one)
    state = attend(queries, one + one_c, state, "attend_1")
    two = after(two, [state[0]])
    rest = two + swap(two)
    outs = attend(queries, rest, state, "attend_2", ys=(0, 1, 2))
    (mine,) = attend(queries, rest, state, "attend_3", ys=(3,), wait=outs[:1])
    o1, o2, o3 = outs
    r2, r1, r3 = shift(o2, "y", 4, -2), shift(o1, "y", 4, -1), shift(o3, "y", 4, -3)
    return combine([mine, r2, r1, r3])


def solution(mesh):
    fine = Mesh(mesh.devices.reshape(2, 2, 8, 4, 2), AXES)
    rows = P(AXES, None)
    return jax.shard_map(
        local, mesh=fine, in_specs=(rows, rows, rows, P(AXES)), out_specs=rows, check_vma=False
    )
```
